32 devices in a mesh: band: 2 (over x), inp: 16 (over z, y, core).
Axes of the slice: x: 2, y: 2, z: 4, core: 2. Of those that a mesh axis runs over, the one named last changes fastest.
Arguments:
- samples: bfloat16 [256, 268288], P(('band', 'inp')), parts along dimension 0, may hold values from -128 to 127, as said below
- taps: int32 [4, 2048], replicated, may hold values from -127 to 127
Outputs:
- visibilities: bfloat16 [64, 2, 128, 128], P(('band', 'inp')), parts along dimension 0
The draws below stay inside these ranges and needn't reach their ends.
There are 2 independent parts, one for each index of `band`. The reference program is written for one: setup_inputs(seed, part) draws one part's arguments, and reference() takes and returns one part's arrays. A program takes and returns all parts, laid end to end along the dimension named above; an argument that names none is the same for every part. Nothing has to cross between parts.
Inputs may be any that keep to these rules, and one draw needn't show every extreme that they name: `samples`: every sample is an integer.
All inputs are finite; a program needn't handle non-finite values.
Results may differ from the reference program's by a relative error of at most 0.0074.
Values may be sent and summed in bfloat16 or wider, within the bound.
A program may use at most 64 MiB of HBM per device.

```python
import math
import jax
import jax.numpy as jnp
from jax import lax

INP_DEV = 8
NFFT = 2048
TAPS = 4
FIRST_CH = 256
SPEC = 128
INPUTS = 128
CHANNELS = 32


def draw_samples(key, part):
    shape = (INPUTS, (SPEC + TAPS - 1) * NFFT)
    values = jax.random.randint(jax.random.fold_in(key, 13), shape, -128, 128)
    return values.astype(jnp.float32).astype(jnp.bfloat16)


def touch_ends(values, key, low, top_value):
    dims = values.shape
    index_at = [jax.random.randint(jax.random.fold_in(key, axis), (), 0, dims[axis]) for axis in range(len(dims))]
    values = values.at[tuple(index_at)].set(low)
    longest = dims.index(max(dims))
    index_at[longest] = (index_at[longest] + 1) % dims[longest]
    return values.at[tuple(index_at)].set(top_value)


def setup_inputs(seed: int = 0, part: int = 0) -> dict:
    keys = jax.random.split(jax.random.key(seed), 3)
    part_splits = jax.random.split(jax.random.fold_in(keys[2], part), 3)
    return {
        "samples": draw_samples(jax.random.fold_in(jax.random.fold_in(keys[2], part), 71), part),
        "taps": touch_ends(jax.random.randint(keys[1], (TAPS, NFFT), -127, 128), jax.random.fold_in(keys[1], 1), -127, 127).astype(jnp.int32),
    }


def band_tables():
    sample_index = jnp.arange(NFFT, dtype=jnp.int32)[:, None]
    channel = FIRST_CH + jnp.arange(CHANNELS, dtype=jnp.int32)[None, :]
    phase = (sample_index * channel % NFFT).astype(jnp.float32) * (2.0 * math.pi / NFFT)
    scale_factor = 2.0 ** (-19)
    cos_table = (jnp.cos(phase) * scale_factor).astype(jnp.bfloat16)
    sin_table = (-jnp.sin(phase) * scale_factor).astype(jnp.bfloat16)
    return (cos_table, sin_table)

def outer_sum(left, right):
    return jnp.dot(left, right.T, preferred_element_type=jnp.float32)

def reference(samples, taps):
    cos_table, sin_table = band_tables()
    tap_values = taps.astype(jnp.float32)
    blocks = samples.reshape(INPUTS // INP_DEV, INP_DEV, SPEC + TAPS - 1, NFFT)

    def channelize(block):
        frames = block.astype(jnp.float32)
        filtered = tap_values[0] * frames[:, 0:SPEC, :]
        for tap_index in range(1, TAPS):
            filtered = filtered + tap_values[tap_index] * frames[:, tap_index:tap_index + SPEC, :]
        flat_rows = filtered.reshape(INP_DEV * SPEC, NFFT).astype(jnp.bfloat16)
        real_volts = jnp.dot(flat_rows, cos_table, preferred_element_type=jnp.float32).astype(jnp.bfloat16)
        imag_volts = jnp.dot(flat_rows, sin_table, preferred_element_type=jnp.float32).astype(jnp.bfloat16)
        return jnp.stack([real_volts, imag_volts]).reshape(2, INP_DEV, SPEC, CHANNELS)
    voltages = lax.map(channelize, blocks)
    voltages = jnp.moveaxis(voltages, 1, 0).reshape(2, INPUTS, SPEC, CHANNELS)
    per_channel = jnp.transpose(voltages, (3, 0, 1, 2))
    norm_factor = 1.0 / math.sqrt(SPEC)

    def correlate(volts):
        real_volts = volts[0]
        imag_volts = volts[1]
        real_part = outer_sum(real_volts, real_volts) + outer_sum(imag_volts, imag_volts)
        imag_part = outer_sum(imag_volts, real_volts) - outer_sum(real_volts, imag_volts)
        return (jnp.stack([real_part, imag_part]) * norm_factor).astype(jnp.bfloat16)
    return lax.map(correlate, per_channel)
```

```python
import functools
import math

import jax
import jax.numpy as jnp
import numpy as np
from jax import lax
from jax.experimental import pallas as pl
from jax.experimental.pallas import tpu as pltpu
from jax.sharding import PartitionSpec as P

CH_DEV = 2
NFFT = 2048
TAPS = 4
FIRST_CH = 256
SPEC = 128
INP_DEV = 8
FRAMES = SPEC + TAPS - 1
BLOCK = 16
COLS = BLOCK * CH_DEV * 2
CHUNKS = ((0, 34), (34, 68), (68, 100), (100, 131))
PAD_ROWS = (FRAMES + 1) * INP_DEV
BLOCK_ROWS = CH_DEV * 2 * INP_DEV


def dft_table(groups):
    n = np.arange(NFFT, dtype=np.int64)[None, :]
    row = np.arange(groups * CH_DEV * 2)[:, None]
    group = row // COLS * BLOCK + row % BLOCK
    part = row // BLOCK % (CH_DEV * 2)
    channel = FIRST_CH + group * CH_DEV + part // 2
    phase = (n * channel % NFFT).astype(np.float32) * np.float32(2.0 * math.pi / NFFT)
    phase = phase.astype(np.float64)
    table = np.where(part % 2 == 0, np.cos(phase), -np.sin(phase)).astype(np.float32)
    return (table * np.float32(2.0**-19)).astype(jnp.bfloat16)


def for_each(count, body):
    if count == 1:
        body(0)
    else:
        pl.loop(0, count)(body)


def kernel(
    groups, samples, taps, table, out,
    x_raw, x, taps_v, table_v, weights, prod, volts, turned, send, recv, stack,
    load_sem, sample_sem, send_sem, recv_sem,
):
    me = lax.axis_index("inp")
    blocks = groups // BLOCK
    taps_copy = pltpu.make_async_copy(taps, taps_v, load_sem.at[0])
    table_copy = pltpu.make_async_copy(table, table_v, load_sem.at[1])
    taps_copy.start()
    table_copy.start()
    loads = []
    for index, (first, last) in enumerate(CHUNKS):
        part = pl.ds(first * NFFT, (last - first) * NFFT)
        loads.append(
            pltpu.make_async_copy(samples.at[:, part], x_raw.at[:, part], sample_sem.at[index])
        )
        loads[-1].start()

    barrier = pltpu.get_barrier_semaphore()

    @pl.loop(1, groups)
    def _(step):
        peer = lax.rem(me + step, groups)
        pl.semaphore_signal(
            barrier, inc=1, device_id={"inp": peer}, device_id_type=pl.DeviceIdType.MESH
        )

    taps_copy.wait()
    table_copy.wait()

    def weigh(b):
        values = table_v[pl.ds(b * COLS, COLS), :].astype(jnp.float32)
        for t in range(TAPS):
            tap = taps_v[t : t + 1, :].astype(jnp.float32)
            weights[b, t * COLS : (t + 1) * COLS, :] = (values * tap).astype(jnp.bfloat16)

    for_each(blocks, weigh)

    for index, (first, last) in enumerate(CHUNKS):
        loads[index].wait()
        for f in range(first, last, 2):
            g = min(f + 1, FRAMES - 1)
            x[f * INP_DEV : (f + 2) * INP_DEV, :] = jnp.concatenate(
                [x_raw[:, f * NFFT : (f + 1) * NFFT], x_raw[:, g * NFFT : (g + 1) * NFFT]], axis=0
            )
        rows = slice(first * INP_DEV, (last + last % 2) * INP_DEV)

        def multiply(b):
            prod[b, rows, :] = lax.dot_general(
                x[rows, :], weights[b], (((1,), (1,)), ((), ())), preferred_element_type=jnp.float32
            )

        for_each(blocks, multiply)

    def turn(b):
        count = SPEC * INP_DEV
        half = prod[b, 0 : count + INP_DEV, 0:128] + prod[b, 16 : count + 24, 128:256]
        volts[...] = half[:count] + pltpu.roll(half[INP_DEV:], COLS, 1)
        lane = lax.broadcasted_iota(jnp.int32, (SPEC, 128), 1)
        for i in range(INP_DEV // 2):
            low = volts[pl.ds(i, SPEC, stride=INP_DEV), :]
            high = volts[pl.ds(i + 4, SPEC, stride=INP_DEV), :]
            pair = jnp.where(lane < COLS, low, pltpu.roll(high, COLS, 1)).T
            for k in range(8):
                to = (k % 4) * INP_DEV * BLOCK + (i + 4 * (k // 4)) * BLOCK
                turned[to : to + BLOCK, :] = pair[k * BLOCK : (k + 1) * BLOCK, :]
        for g in range(BLOCK):
            send[b * BLOCK + g] = turned[pl.ds(g, BLOCK_ROWS, stride=BLOCK), :].astype(jnp.bfloat16)

    for_each(blocks, turn)

    pl.semaphore_wait(barrier, groups - 1)

    def transfer(peer):
        return pltpu.make_async_remote_copy(
            src_ref=send.at[peer],
            dst_ref=recv.at[me],
            send_sem=send_sem.at[peer],
            recv_sem=recv_sem.at[me],
            device_id={"inp": peer},
            device_id_type=pl.DeviceIdType.MESH,
        )

    @pl.loop(1, groups)
    def _(step):
        transfer(lax.rem(me + step, groups)).start()

    recv[me] = send[me]

    @pl.loop(1, groups)
    def _(step):
        peer = lax.rem(me + groups - step, groups)
        pltpu.make_async_remote_copy(
            src_ref=send.at[peer],
            dst_ref=recv.at[peer],
            send_sem=send_sem.at[peer],
            recv_sem=recv_sem.at[peer],
            device_id={"inp": peer},
            device_id_type=pl.DeviceIdType.MESH,
        ).wait_recv()

    inputs = groups * INP_DEV
    norm = 1.0 / math.sqrt(SPEC)
    for q in range(CH_DEV):
        for r in range(2):
            at = (2 * q + r) * INP_DEV
            values = recv[:, at : at + INP_DEV, :].astype(jnp.float32).reshape(inputs, SPEC)
            stack[q, 0, :, r * SPEC : (r + 1) * SPEC] = values.astype(jnp.bfloat16)
            turned_part = values if r == 1 else -values
            stack[q, 1, :, (1 - r) * SPEC : (2 - r) * SPEC] = turned_part.astype(jnp.bfloat16)

    def correlate(tile):
        rows = pl.ds(tile * SPEC, SPEC)
        for q in range(CH_DEV):
            for r in range(2):
                product = lax.dot_general(
                    stack[q, r, rows, :], stack[q, 0], (((1,), (1,)), ((), ())),
                    preferred_element_type=jnp.float32,
                )
                out[q, r, rows, :] = (product * norm).astype(jnp.bfloat16)

    for_each(inputs // SPEC, correlate)

    @pl.loop(1, groups)
    def _(step):
        transfer(lax.rem(me + step, groups)).wait_send()


def per_device(samples, taps):
    groups = lax.axis_size("inp")
    blocks = groups // BLOCK
    inputs = groups * INP_DEV
    table = jnp.asarray(dft_table(groups))
    anywhere = pl.BlockSpec(memory_space=pl.ANY)
    bf16, f32 = jnp.bfloat16, jnp.float32
    return pl.pallas_call(
        functools.partial(kernel, groups),
        out_shape=jax.ShapeDtypeStruct((CH_DEV, 2, inputs, inputs), bf16),
        in_specs=[anywhere] * 3,
        out_specs=pl.BlockSpec(memory_space=pltpu.VMEM),
        scratch_shapes=[
            pltpu.VMEM((INP_DEV, FRAMES * NFFT), bf16),
            pltpu.VMEM((PAD_ROWS, NFFT), bf16),
            pltpu.VMEM((TAPS, NFFT), jnp.int32),
            pltpu.VMEM((groups * CH_DEV * 2, NFFT), bf16),
            pltpu.VMEM((blocks, TAPS * COLS, NFFT), bf16),
            pltpu.VMEM((blocks, PAD_ROWS, TAPS * COLS), f32),
            pltpu.VMEM((SPEC * INP_DEV, 128), f32),
            pltpu.VMEM((COLS * INP_DEV, SPEC), f32),
            pltpu.VMEM((groups, BLOCK_ROWS, SPEC), bf16),
            pltpu.VMEM((groups, BLOCK_ROWS, SPEC), bf16),
            pltpu.VMEM((CH_DEV, 2, inputs, 2 * SPEC), bf16),
            pltpu.SemaphoreType.DMA((2,)),
            pltpu.SemaphoreType.DMA((len(CHUNKS),)),
            pltpu.SemaphoreType.DMA((groups,)),
            pltpu.SemaphoreType.DMA((groups,)),
        ],
        compiler_params=pltpu.CompilerParams(
            collective_id=0, has_side_effects=True, vmem_limit_bytes=60 * 2**20
        ),
        name="correlator",
    )(samples, taps, table)


def solution(mesh):
    placed = (P(("band", "inp"), None), P())
    return jax.shard_map(
        per_device,
        mesh=mesh,
        in_specs=placed,
        out_specs=P(("band", "inp"), None, None, None),
        check_vma=False,
    )
```

```python
import functools
import math

import jax
import jax.numpy as jnp
import numpy as np
from jax import lax
from jax.experimental import pallas as pl
from jax.experimental.pallas import tpu as pltpu
from jax.sharding import PartitionSpec as P

CH_DEV = 2
NFFT = 2048
TAPS = 4
FIRST_CH = 256
SPEC = 128
INP_DEV = 8
FRAMES = SPEC + TAPS - 1
BLOCK = 16
COLS = BLOCK * CH_DEV * 2
CHUNKS = ((0, 34), (34, 68), (68, 100), (100, 131))
PAD_ROWS = (FRAMES + 1) * INP_DEV
BLOCK_ROWS = CH_DEV * 2 * INP_DEV


def dft_table(groups):
    n = np.arange(NFFT, dtype=np.int64)[None, :, None]
    block = np.arange(groups // BLOCK)[:, None, None]
    column = np.arange(2 * COLS)[None, None, :] % COLS
    part = column // BLOCK
    channel = FIRST_CH + (block * BLOCK + column % BLOCK) * CH_DEV + part // 2
    phase = (n * channel % NFFT).astype(np.float32) * np.float32(2.0 * math.pi / NFFT)
    phase = phase.astype(np.float64)
    table = np.where(part % 2 == 0, np.cos(phase), -np.sin(phase)).astype(np.float32)
    return (table * np.float32(2.0**-19)).astype(jnp.bfloat16)


def for_each(count, body):
    if count == 1:
        body(0)
    else:
        pl.loop(0, count)(body)


def kernel(
    groups, samples, taps, table, recv,
    x_raw, x, taps_v, table_v, weights, prod, volts, turned, send, own_sem,
    load_sem, sample_sem, send_sem, recv_sem,
):
    me = lax.axis_index("inp")
    blocks = groups // BLOCK
    taps_copy = pltpu.make_async_copy(taps, taps_v, load_sem.at[0])
    table_copy = pltpu.make_async_copy(table, table_v, load_sem.at[1])
    taps_copy.start()
    table_copy.start()
    loads = []
    for index, (first, last) in enumerate(CHUNKS):
        part = pl.ds(first * NFFT, (last - first) * NFFT)
        loads.append(
            pltpu.make_async_copy(samples.at[:, part], x_raw.at[:, part], sample_sem.at[index])
        )
        loads[-1].start()

    barrier = pltpu.get_barrier_semaphore()

    @pl.loop(1, groups)
    def _(step):
        peer = lax.rem(me + step, groups)
        pl.semaphore_signal(
            barrier, inc=1, device_id={"inp": peer}, device_id_type=pl.DeviceIdType.MESH
        )

    taps_copy.wait()
    table_copy.wait()

    width = TAPS * COLS
    tap_rows = taps_v[...].astype(jnp.float32)
    tap_rows = jnp.concatenate([tap_rows, jnp.zeros_like(tap_rows)], axis=0).astype(jnp.bfloat16)
    tap_of = lax.broadcasted_iota(jnp.int32, (2 * TAPS, width), 1) // COLS
    spread = (tap_of == lax.broadcasted_iota(jnp.int32, (2 * TAPS, width), 0)).astype(jnp.bfloat16)

    def weigh(b):
        spread_taps = lax.dot_general(
            tap_rows, spread, (((0,), (0,)), ((), ())), preferred_element_type=jnp.float32
        )
        values = table_v[b].astype(jnp.float32)
        for h in range(2):
            lanes = slice(h * 2 * COLS, (h + 1) * 2 * COLS)
            weights[b, :, lanes] = (values * spread_taps[:, lanes]).astype(jnp.bfloat16)

    for_each(blocks, weigh)

    for index, (first, last) in enumerate(CHUNKS):
        loads[index].wait()
        for f in range(first, last, 2):
            g = min(f + 1, FRAMES - 1)
            x[f * INP_DEV : (f + 2) * INP_DEV, :] = jnp.concatenate(
                [x_raw[:, f * NFFT : (f + 1) * NFFT], x_raw[:, g * NFFT : (g + 1) * NFFT]], axis=0
            )
        if index % 2 == 0:
            continue
        rows = slice(CHUNKS[index - 1][0] * INP_DEV, (last + last % 2) * INP_DEV)

        def multiply(b):
            prod[b, rows, :] = jnp.dot(
                x[rows, :], weights[b], preferred_element_type=jnp.float32
            )

        for_each(blocks, multiply)

    def turn(b):
        count = SPEC * INP_DEV
        half = prod[b, 0 : count + INP_DEV, 0:128] + prod[b, 16 : count + 24, 128:256]
        volts[...] = half[:count] + pltpu.roll(half[INP_DEV:], COLS, 1)
        lane = lax.broadcasted_iota(jnp.int32, (SPEC, 128), 1)
        for i in range(INP_DEV // 2):
            low = volts[pl.ds(i, SPEC, stride=INP_DEV), :]
            high = volts[pl.ds(i + 4, SPEC, stride=INP_DEV), :]
            pair = jnp.where(lane < COLS, low, pltpu.roll(high, COLS, 1)).T
            for k in range(8):
                to = (k % 4) * INP_DEV * BLOCK + (i + 4 * (k // 4)) * BLOCK
                turned[to : to + BLOCK, :] = pair[k * BLOCK : (k + 1) * BLOCK, :]
        for g in range(BLOCK):
            send[b * BLOCK + g] = turned[pl.ds(g, BLOCK_ROWS, stride=BLOCK), :].astype(jnp.bfloat16)

    for_each(blocks, turn)

    pl.semaphore_wait(barrier, groups - 1)

    def transfer(peer):
        return pltpu.make_async_remote_copy(
            src_ref=send.at[peer],
            dst_ref=recv.at[me],
            send_sem=send_sem.at[peer],
            recv_sem=recv_sem.at[me],
            device_id={"inp": peer},
            device_id_type=pl.DeviceIdType.MESH,
        )

    @pl.loop(1, groups)
    def _(step):
        transfer(lax.rem(me + step, groups)).start()

    own = pltpu.make_async_copy(send.at[me], recv.at[me], own_sem)
    own.start()

    @pl.loop(1, groups)
    def _(step):
        peer = lax.rem(me + groups - step, groups)
        pltpu.make_async_remote_copy(
            src_ref=send.at[peer],
            dst_ref=recv.at[peer],
            send_sem=send_sem.at[peer],
            recv_sem=recv_sem.at[peer],
            device_id={"inp": peer},
            device_id_type=pl.DeviceIdType.MESH,
        ).wait_recv()

    own.wait()

    @pl.loop(1, groups)
    def _(step):
        transfer(lax.rem(me + step, groups)).wait_send()


def correlate_kernel(recv, out, stack):
    inputs = recv.shape[0] * INP_DEV
    norm = 1.0 / math.sqrt(SPEC)
    for q in range(CH_DEV):
        for r in range(2):
            at = (2 * q + r) * INP_DEV
            values = recv[:, at : at + INP_DEV, :].astype(jnp.float32).reshape(inputs, SPEC)
            stack[q, 0, :, r * SPEC : (r + 1) * SPEC] = values.astype(jnp.bfloat16)
            turned_part = values if r == 1 else -values
            stack[q, 1, :, (1 - r) * SPEC : (2 - r) * SPEC] = turned_part.astype(jnp.bfloat16)

    def correlate(tile):
        rows = pl.ds(tile * SPEC, SPEC)
        for q in range(CH_DEV):
            for r in range(2):
                product = lax.dot_general(
                    stack[q, r, rows, :], stack[q, 0], (((1,), (1,)), ((), ())),
                    preferred_element_type=jnp.float32,
                )
                out[q, r, rows, :] = (product * norm).astype(jnp.bfloat16)

    for_each(inputs // SPEC, correlate)


def per_device(samples, taps):
    groups = lax.axis_size("inp")
    blocks = groups // BLOCK
    inputs = groups * INP_DEV
    table = jnp.asarray(dft_table(groups))
    anywhere = pl.BlockSpec(memory_space=pl.ANY)
    bf16, f32 = jnp.bfloat16, jnp.float32
    gathered = pl.pallas_call(
        functools.partial(kernel, groups),
        out_shape=jax.ShapeDtypeStruct((groups, BLOCK_ROWS, SPEC), bf16),
        in_specs=[anywhere] * 3,
        out_specs=anywhere,
        scratch_shapes=[
            pltpu.VMEM((INP_DEV, FRAMES * NFFT), bf16),
            pltpu.VMEM((PAD_ROWS, NFFT), bf16),
            pltpu.VMEM((TAPS, NFFT), jnp.int32),
            pltpu.VMEM((blocks, NFFT, 2 * COLS), bf16),
            pltpu.VMEM((blocks, NFFT, TAPS * COLS), bf16),
            pltpu.VMEM((blocks, PAD_ROWS, TAPS * COLS), f32),
            pltpu.VMEM((SPEC * INP_DEV, 128), f32),
            pltpu.VMEM((COLS * INP_DEV, SPEC), f32),
            pltpu.VMEM((groups, BLOCK_ROWS, SPEC), bf16),
            pltpu.SemaphoreType.DMA,
            pltpu.SemaphoreType.DMA((2,)),
            pltpu.SemaphoreType.DMA((len(CHUNKS),)),
            pltpu.SemaphoreType.DMA((groups,)),
            pltpu.SemaphoreType.DMA((groups,)),
        ],
        compiler_params=pltpu.CompilerParams(
            collective_id=0, has_side_effects=True, vmem_limit_bytes=60 * 2**20
        ),
        name="channelize",
    )(samples, taps, table)
    return pl.pallas_call(
        correlate_kernel,
        out_shape=jax.ShapeDtypeStruct((CH_DEV, 2, inputs, inputs), bf16),
        in_specs=[pl.BlockSpec(memory_space=pltpu.VMEM)],
        out_specs=pl.BlockSpec(memory_space=pltpu.VMEM),
        scratch_shapes=[pltpu.VMEM((CH_DEV, 2, inputs, 2 * SPEC), bf16)],
        compiler_params=pltpu.CompilerParams(vmem_limit_bytes=60 * 2**20),
        name="correlate",
    )(gathered)


def solution(mesh):
    placed = (P(("band", "inp"), None), P())
    return jax.shard_map(
        per_device,
        mesh=mesh,
        in_specs=placed,
        out_specs=P(("band", "inp"), None, None, None),
        check_vma=False,
    )
```

```python
import functools
import math

import jax
import jax.numpy as jnp
import numpy as np
from jax import lax
from jax.experimental import pallas as pl
from jax.experimental.pallas import tpu as pltpu
from jax.sharding import PartitionSpec as P

CH_DEV = 2
NFFT = 2048
TAPS = 4
FIRST_CH = 256
SPEC = 128
INP_DEV = 8
FRAMES = SPEC + TAPS - 1
BLOCK = 16
COLS = BLOCK * CH_DEV * 2
HALF = SPEC // 2
HALF_FRAMES = 68
HALF_ROWS = HALF_FRAMES * INP_DEV
LATE_FRAMES = FRAMES - HALF_FRAMES
LOADS = ((0, 32), (32, LATE_FRAMES - 32))
BLOCK_ROWS = CH_DEV * INP_DEV


def dft_table(groups):
    n = np.arange(NFFT, dtype=np.int64)[None, :, None]
    block = np.arange(groups // BLOCK)[:, None, None]
    column = np.arange(2 * COLS)[None, None, :] % COLS
    part = column // BLOCK
    channel = FIRST_CH + (block * BLOCK + column % BLOCK) * CH_DEV + part % CH_DEV
    phase = (n * channel % NFFT).astype(np.float32) * np.float32(2.0 * math.pi / NFFT)
    phase = phase.astype(np.float64)
    table = np.where(part < CH_DEV, np.cos(phase), -np.sin(phase)).astype(np.float32)
    return (table * np.float32(2.0**-19)).astype(jnp.bfloat16)


def for_each(count, body):
    if count == 1:
        body(0)
    else:
        pl.loop(0, count)(body)


def kernel(
    groups, samples, taps, table, recv,
    x_raw, x, taps_v, table_v, weights, prod, volts, turned, send,
    load_sem, sample_sem, own_sem, send_sem, recv_sem,
):
    me = lax.axis_index("inp")
    blocks = groups // BLOCK
    taps_copy = pltpu.make_async_copy(taps, taps_v, load_sem.at[0])
    table_copy = pltpu.make_async_copy(table, table_v, load_sem.at[1])
    taps_copy.start()
    table_copy.start()

    def load(first, count, sem):
        part = pl.ds(first * NFFT, count * NFFT)
        return pltpu.make_async_copy(samples.at[:, part], x_raw.at[:, part], sem)

    extra = load(LATE_FRAMES, HALF_FRAMES - LATE_FRAMES, load_sem.at[2])
    for h in range(2):
        for index, (first, count) in enumerate(LOADS):
            load(h * HALF_FRAMES + first, count, sample_sem.at[h, index]).start()
        if h == 0:
            extra.start()

    barrier = pltpu.get_barrier_semaphore()

    @pl.loop(1, groups)
    def _(step):
        peer = lax.rem(me + step, groups)
        pl.semaphore_signal(
            barrier, inc=1, device_id={"inp": peer}, device_id_type=pl.DeviceIdType.MESH
        )

    width = TAPS * COLS
    tap_of = lax.broadcasted_iota(jnp.int32, (2 * TAPS, width), 1) // COLS
    spread = (tap_of == lax.broadcasted_iota(jnp.int32, (2 * TAPS, width), 0)).astype(jnp.bfloat16)
    taps_copy.wait()
    table_copy.wait()

    @pl.loop(0, NFFT // 512)
    def _(tile):
        rows = pl.ds(pl.multiple_of(tile * 512, 512), 512)
        tap_rows = taps_v[:, rows].astype(jnp.float32)
        tap_rows = jnp.concatenate([tap_rows, jnp.zeros_like(tap_rows)], axis=0)
        spread_taps = lax.dot_general(
            tap_rows.astype(jnp.bfloat16), spread, (((0,), (0,)), ((), ())),
            preferred_element_type=jnp.float32,
        )

        def weigh(b):
            values = table_v[b, rows, :].astype(jnp.float32)
            for h in range(2):
                lanes = slice(h * 2 * COLS, (h + 1) * 2 * COLS)
                weights[b, rows, lanes] = (values * spread_taps[:, lanes]).astype(jnp.bfloat16)

        for_each(blocks, weigh)

    extra.wait()

    def transfer(peer, slot, h):
        return pltpu.make_async_remote_copy(
            src_ref=send.at[peer, h],
            dst_ref=recv.at[slot, h],
            send_sem=send_sem.at[h, peer],
            recv_sem=recv_sem.at[h, slot],
            device_id={"inp": peer},
            device_id_type=pl.DeviceIdType.MESH,
        )

    def own(h):
        return pltpu.make_async_copy(send.at[me, h], recv.at[me, h], own_sem.at[h])

    @pl.loop(0, 2)
    def _(h):
        for index, (first, count) in enumerate(LOADS):
            load(h * HALF_FRAMES + first, count, sample_sem.at[h, index]).wait()

        @pl.loop(0, HALF_FRAMES // 4)
        def _(quad):
            for pair in range(2):
                f = quad * 4 + pair * 2
                frames = [
                    x_raw[:, pl.ds(pl.multiple_of((h * HALF_FRAMES + f + k) * NFFT, NFFT), NFFT)]
                    for k in range(2)
                ]
                rows = pl.ds(pl.multiple_of(f * INP_DEV, 16), 16)
                x[rows, :] = jnp.concatenate(frames, axis=0)

        def multiply(b):
            rows = pl.ds(pl.multiple_of(h * HALF_ROWS, HALF_ROWS), HALF_ROWS)
            prod[b, rows, :] = jnp.dot(x[...], weights[b], preferred_element_type=jnp.float32)

        for_each(blocks, multiply)

        def turn(b):
            count = HALF * INP_DEV
            start = pl.multiple_of(h * count, count)
            half = (
                prod[b, pl.ds(start, count + INP_DEV), 0:128]
                + prod[b, pl.ds(start + 2 * INP_DEV, count + INP_DEV), 128:256]
            )
            volts[...] = half[:count] + pltpu.roll(half[INP_DEV:], COLS, 1)
            low_lanes = lax.broadcasted_iota(jnp.int32, (HALF, 128), 1) < COLS
            for p in range(2):
                rows = []
                for ia in range(2):
                    i = 4 * ia + 2 * p
                    low = volts[pl.ds(i, HALF, stride=INP_DEV), :]
                    high = volts[pl.ds(i + 1, HALF, stride=INP_DEV), :]
                    rows.append(jnp.where(low_lanes, low, pltpu.roll(high, COLS, 1)))
                pair = jnp.concatenate(rows, axis=0).T
                for k in range(8):
                    to = ((k % 4) * 4 + 2 * p + k // 4) * BLOCK
                    turned[to : to + BLOCK, :] = pair[k * BLOCK : (k + 1) * BLOCK, :]
            first = lax.broadcasted_iota(jnp.int32, (INP_DEV, 128), 1) < HALF
            for g in range(BLOCK):
                real = turned[pl.ds(g, 8, stride=BLOCK), :]
                imag = turned[pl.ds(8 * BLOCK + g, 8, stride=BLOCK), :]
                send[b * BLOCK + g, h] = jnp.concatenate(
                    [
                        jnp.where(first, real, pltpu.roll(imag, HALF, 1)),
                        jnp.where(first, pltpu.roll(real, HALF, 1), imag),
                    ],
                    axis=0,
                ).astype(jnp.bfloat16)

        for_each(blocks, turn)

        @pl.when(h == 0)
        def _():
            pl.semaphore_wait(barrier, groups - 1)

        @pl.loop(1, groups)
        def _(step):
            transfer(lax.rem(me + step, groups), me, h).start()

        own(h).start()

    for h in range(2):

        @pl.loop(1, groups)
        def _(step):
            peer = lax.rem(me + groups - step, groups)
            transfer(peer, peer, h).wait_recv()

    for h in range(2):
        own(h).wait()

        @pl.loop(1, groups)
        def _(step):
            transfer(lax.rem(me + step, groups), me, h).wait_send()


def correlate_kernel(recv, out, stack):
    inputs = recv.shape[0] * INP_DEV
    norm = 1.0 / math.sqrt(SPEC)
    shape = (recv.shape[0], INP_DEV, 128)
    upper = lax.broadcasted_iota(jnp.int32, shape, 1) < 4
    first = lax.broadcasted_iota(jnp.int32, (inputs, 128), 1) < HALF
    for h in range(2):
        lanes = slice(h * 128, (h + 1) * 128)
        early = recv[:, h, 0:INP_DEV, :].astype(jnp.float32)
        late = recv[:, h, INP_DEV:, :].astype(jnp.float32)
        by_channel = (
            jnp.where(upper, early, pltpu.roll(late, 4, 1)),
            jnp.where(upper, pltpu.roll(early, 4, 1), late),
        )
        for q in range(CH_DEV):
            values = by_channel[q].reshape(inputs, 128)
            rolled = pltpu.roll(values, HALF, 1)
            stack[q, 0, :, lanes] = values.astype(jnp.bfloat16)
            stack[q, 1, :, lanes] = jnp.where(first, rolled, -rolled).astype(jnp.bfloat16)

    def correlate(tile):
        rows = pl.ds(tile * 128, 128)
        for q in range(CH_DEV):
            for r in range(2):
                product = lax.dot_general(
                    stack[q, r, rows, :], stack[q, 0], (((1,), (1,)), ((), ())),
                    preferred_element_type=jnp.float32,
                )
                out[q, r, rows, :] = (product * norm).astype(jnp.bfloat16)

    for_each(inputs // 128, correlate)


def per_device(samples, taps):
    groups = lax.axis_size("inp")
    blocks = groups // BLOCK
    inputs = groups * INP_DEV
    table = jnp.asarray(dft_table(groups))
    anywhere = pl.BlockSpec(memory_space=pl.ANY)
    bf16, f32 = jnp.bfloat16, jnp.float32
    gathered = pl.pallas_call(
        functools.partial(kernel, groups),
        out_shape=jax.ShapeDtypeStruct((groups, 2, BLOCK_ROWS, 128), bf16),
        in_specs=[anywhere] * 3,
        out_specs=anywhere,
        scratch_shapes=[
            pltpu.VMEM((INP_DEV, 2 * HALF_FRAMES * NFFT), bf16),
            pltpu.VMEM((HALF_ROWS, NFFT), bf16),
            pltpu.VMEM((TAPS, NFFT), jnp.int32),
            pltpu.VMEM((blocks, NFFT, 2 * COLS), bf16),
            pltpu.VMEM((blocks, NFFT, TAPS * COLS), bf16),
            pltpu.VMEM((blocks, 2 * HALF_ROWS, TAPS * COLS), f32),
            pltpu.VMEM((HALF * INP_DEV, 128), f32),
            pltpu.VMEM((BLOCK_ROWS * BLOCK, 128), f32),
            pltpu.VMEM((groups, 2, BLOCK_ROWS, 128), bf16),
            pltpu.SemaphoreType.DMA((3,)),
            pltpu.SemaphoreType.DMA((2, len(LOADS))),
            pltpu.SemaphoreType.DMA((2,)),
            pltpu.SemaphoreType.DMA((2, groups)),
            pltpu.SemaphoreType.DMA((2, groups)),
        ],
        compiler_params=pltpu.CompilerParams(
            collective_id=0, has_side_effects=True, vmem_limit_bytes=60 * 2**20
        ),
        name="channelize",
    )(samples, taps, table)
    return pl.pallas_call(
        correlate_kernel,
        out_shape=jax.ShapeDtypeStruct((CH_DEV, 2, inputs, inputs), bf16),
        in_specs=[pl.BlockSpec(memory_space=pltpu.VMEM)],
        out_specs=pl.BlockSpec(memory_space=pltpu.VMEM),
        scratch_shapes=[pltpu.VMEM((CH_DEV, 2, inputs, 2 * SPEC), bf16)],
        compiler_params=pltpu.CompilerParams(vmem_limit_bytes=60 * 2**20),
        name="correlate",
    )(gathered)


def solution(mesh):
    placed = (P(("band", "inp"), None), P())
    return jax.shard_map(
        per_device,
        mesh=mesh,
        in_specs=placed,
        out_specs=P(("band", "inp"), None, None, None),
        check_vma=False,
    )
```

```python
import functools
import math

import jax
import jax.numpy as jnp
import numpy as np
from jax import lax
from jax.experimental import pallas as pl
from jax.experimental.pallas import tpu as pltpu
from jax.sharding import PartitionSpec as P

CH_DEV = 2
NFFT = 2048
TAPS = 4
FIRST_CH = 256
SPEC = 128
INP_DEV = 8
FRAMES = SPEC + TAPS - 1
BLOCK = 16
COLS = BLOCK * CH_DEV * 2
HALF = SPEC // 2
HALF_FRAMES = 68
HALF_ROWS = HALF_FRAMES * INP_DEV
LATE_FRAMES = FRAMES - HALF_FRAMES
LOADS = ((0, 32), (32, LATE_FRAMES - 32))
BLOCK_ROWS = CH_DEV * INP_DEV


def dft_table(groups):
    n = np.arange(NFFT, dtype=np.int64)[None, :, None]
    block = np.arange(groups // BLOCK)[:, None, None]
    column = np.arange(2 * COLS)[None, None, :] % COLS
    part = column // BLOCK
    channel = FIRST_CH + (block * BLOCK + column % BLOCK) * CH_DEV + part % CH_DEV
    phase = (n * channel % NFFT).astype(np.float32) * np.float32(2.0 * math.pi / NFFT)
    phase = phase.astype(np.float64)
    table = np.where(part < CH_DEV, np.cos(phase), -np.sin(phase)).astype(np.float32)
    return (table * np.float32(2.0**-19)).astype(jnp.bfloat16)


def for_each(count, body):
    if count == 1:
        body(0)
    else:
        pl.loop(0, count)(body)


def for_each_peer(groups, body):
    if groups <= BLOCK:
        for step in range(1, groups):
            body(step)
    else:
        pl.loop(1, groups)(body)


def kernel(
    groups, samples, taps, table, recv,
    x_raw, x, taps_v, table_v, weights, prod, volts, turned, send,
    load_sem, sample_sem, own_sem, send_sem, recv_sem,
):
    me = lax.axis_index("inp")
    blocks = groups // BLOCK
    taps_copy = pltpu.make_async_copy(taps, taps_v, load_sem.at[0])
    table_copy = pltpu.make_async_copy(table, table_v, load_sem.at[1])
    taps_copy.start()
    table_copy.start()

    def load(first, count, sem):
        part = pl.ds(first * NFFT, count * NFFT)
        return pltpu.make_async_copy(samples.at[:, part], x_raw.at[:, part], sem)

    extra = load(LATE_FRAMES, HALF_FRAMES - LATE_FRAMES, load_sem.at[2])
    for h in range(2):
        for index, (first, count) in enumerate(LOADS):
            load(h * HALF_FRAMES + first, count, sample_sem.at[h, index]).start()
        if h == 0:
            extra.start()

    barrier = pltpu.get_barrier_semaphore()

    def greet(step):
        peer = lax.rem(me + step, groups)
        pl.semaphore_signal(
            barrier, inc=1, device_id={"inp": peer}, device_id_type=pl.DeviceIdType.MESH
        )

    for_each_peer(groups, greet)

    width = TAPS * COLS
    tap_of = lax.broadcasted_iota(jnp.int32, (2 * TAPS, width), 1) // COLS
    spread = (tap_of == lax.broadcasted_iota(jnp.int32, (2 * TAPS, width), 0)).astype(jnp.bfloat16)
    taps_copy.wait()
    table_copy.wait()

    tap_rows = taps_v[...].astype(jnp.float32)
    tap_rows = jnp.concatenate([tap_rows, jnp.zeros_like(tap_rows)], axis=0).astype(jnp.bfloat16)
    spread_taps = lax.dot_general(
        tap_rows, spread, (((0,), (0,)), ((), ())), preferred_element_type=jnp.float32
    )

    def weigh(b):
        values = table_v[b].astype(jnp.float32)
        for h in range(2):
            lanes = slice(h * 2 * COLS, (h + 1) * 2 * COLS)
            weights[b, :, lanes] = (values * spread_taps[:, lanes]).astype(jnp.bfloat16)

    for_each(blocks, weigh)

    extra.wait()

    def transfer(peer, source, target):
        return pltpu.make_async_remote_copy(
            src_ref=source,
            dst_ref=target,
            send_sem=send_sem,
            recv_sem=recv_sem,
            device_id={"inp": peer},
            device_id_type=pl.DeviceIdType.MESH,
        )

    def own(h):
        return pltpu.make_async_copy(send.at[me, h], recv.at[me, h], own_sem.at[h])

    @pl.loop(0, 2)
    def _(h):
        for index, (first, count) in enumerate(LOADS):
            load(h * HALF_FRAMES + first, count, sample_sem.at[h, index]).wait()

        for column in range(0, NFFT, 256):
            for f in range(0, HALF_FRAMES, 2):
                frames = []
                for k in range(2):
                    start = pl.multiple_of((h * HALF_FRAMES + f + k) * NFFT + column, 256)
                    frames.append(x_raw[:, pl.ds(start, 256)])
                x[f * INP_DEV : (f + 2) * INP_DEV, column : column + 256] = jnp.concatenate(
                    frames, axis=0
                )

        def multiply(b):
            rows = pl.ds(pl.multiple_of(h * HALF_ROWS, HALF_ROWS), HALF_ROWS)
            prod[b, rows, :] = jnp.dot(x[...], weights[b], preferred_element_type=jnp.float32)

        for_each(blocks, multiply)

        def turn(b):
            count = HALF * INP_DEV
            start = pl.multiple_of(h * count, count)
            half = (
                prod[b, pl.ds(start, count + INP_DEV), 0:128]
                + prod[b, pl.ds(start + 2 * INP_DEV, count + INP_DEV), 128:256]
            )
            volts[...] = half[:count] + pltpu.roll(half[INP_DEV:], COLS, 1)
            low_lanes = lax.broadcasted_iota(jnp.int32, (HALF, 128), 1) < COLS
            for p in range(2):
                rows = []
                for ia in range(2):
                    i = 4 * ia + 2 * p
                    low = volts[pl.ds(i, HALF, stride=INP_DEV), :]
                    high = volts[pl.ds(i + 1, HALF, stride=INP_DEV), :]
                    rows.append(jnp.where(low_lanes, low, pltpu.roll(high, COLS, 1)))
                pair = jnp.concatenate(rows, axis=0).T
                for k in range(8):
                    to = ((k % 4) * 4 + 2 * p + k // 4) * BLOCK
                    turned[to : to + BLOCK, :] = pair[k * BLOCK : (k + 1) * BLOCK, :]
            first = lax.broadcasted_iota(jnp.int32, (INP_DEV, 128), 1) < HALF
            for g in range(BLOCK):
                real = turned[pl.ds(g, 8, stride=BLOCK), :]
                imag = turned[pl.ds(8 * BLOCK + g, 8, stride=BLOCK), :]
                send[b * BLOCK + g, h] = jnp.concatenate(
                    [
                        jnp.where(first, real, pltpu.roll(imag, HALF, 1)),
                        jnp.where(first, pltpu.roll(real, HALF, 1), imag),
                    ],
                    axis=0,
                ).astype(jnp.bfloat16)

        for_each(blocks, turn)

        @pl.when(h == 0)
        def _():
            pl.semaphore_wait(barrier, groups - 1)

        def start(step):
            peer = lax.rem(me + step, groups)
            transfer(peer, send.at[peer, h], recv.at[me, h]).start()

        for_each_peer(groups, start)

        own(h).start()

    for h in range(2):
        own(h).wait()
    others = pl.ds(0, groups - 1)
    everything = transfer(lax.rem(me + 1, groups), send.at[others], recv.at[others])
    everything.wait_recv()
    everything.wait_send()


def correlate_kernel(recv, out, stack):
    inputs = recv.shape[0] * INP_DEV
    norm = 1.0 / math.sqrt(SPEC)
    shape = (recv.shape[0], INP_DEV, 128)
    upper = lax.broadcasted_iota(jnp.int32, shape, 1) < 4
    first = lax.broadcasted_iota(jnp.int32, (inputs, 128), 1) < HALF
    for h in range(2):
        lanes = slice(h * 128, (h + 1) * 128)
        early = recv[:, h, 0:INP_DEV, :].astype(jnp.float32)
        late = recv[:, h, INP_DEV:, :].astype(jnp.float32)
        by_channel = (
            jnp.where(upper, early, pltpu.roll(late, 4, 1)),
            jnp.where(upper, pltpu.roll(early, 4, 1), late),
        )
        for q in range(CH_DEV):
            values = by_channel[q].reshape(inputs, 128)
            rolled = pltpu.roll(values, HALF, 1)
            stack[q, 0, :, lanes] = values.astype(jnp.bfloat16)
            stack[q, 1, :, lanes] = jnp.where(first, rolled, -rolled).astype(jnp.bfloat16)

    def correlate(tile):
        rows = pl.ds(tile * 128, 128)
        for q in range(CH_DEV):
            for r in range(2):
                product = lax.dot_general(
                    stack[q, r, rows, :], stack[q, 0], (((1,), (1,)), ((), ())),
                    preferred_element_type=jnp.float32,
                )
                out[q, r, rows, :] = (product * norm).astype(jnp.bfloat16)

    for_each(inputs // 128, correlate)


def per_device(samples, taps):
    groups = lax.axis_size("inp")
    blocks = groups // BLOCK
    inputs = groups * INP_DEV
    table = jnp.asarray(dft_table(groups))
    anywhere = pl.BlockSpec(memory_space=pl.ANY)
    bf16, f32 = jnp.bfloat16, jnp.float32
    gathered = pl.pallas_call(
        functools.partial(kernel, groups),
        out_shape=pltpu.VMEM((groups, 2, BLOCK_ROWS, 128), bf16),
        in_specs=[pl.BlockSpec(memory_space=pltpu.HBM)] * 3,
        out_specs=pl.BlockSpec(memory_space=pltpu.VMEM),
        scratch_shapes=[
            pltpu.VMEM((INP_DEV, 2 * HALF_FRAMES * NFFT), bf16),
            pltpu.VMEM((HALF_ROWS, NFFT), bf16),
            pltpu.VMEM((TAPS, NFFT), jnp.int32),
            pltpu.VMEM((blocks, NFFT, 2 * COLS), bf16),
            pltpu.VMEM((blocks, NFFT, TAPS * COLS), bf16),
            pltpu.VMEM((blocks, 2 * HALF_ROWS, TAPS * COLS), f32),
            pltpu.VMEM((HALF * INP_DEV, 128), f32),
            pltpu.VMEM((BLOCK_ROWS * BLOCK, 128), f32),
            pltpu.VMEM((groups, 2, BLOCK_ROWS, 128), bf16),
            pltpu.SemaphoreType.DMA((3,)),
            pltpu.SemaphoreType.DMA((2, len(LOADS))),
            pltpu.SemaphoreType.DMA((2,)),
            pltpu.SemaphoreType.DMA,
            pltpu.SemaphoreType.DMA,
        ],
        compiler_params=pltpu.CompilerParams(
            collective_id=0, has_side_effects=True, vmem_limit_bytes=58 * 2**20
        ),
        name="channelize",
    )(samples, taps, table)
    return pl.pallas_call(
        correlate_kernel,
        out_shape=jax.ShapeDtypeStruct((CH_DEV, 2, inputs, inputs), bf16),
        in_specs=[pl.BlockSpec(memory_space=pltpu.VMEM)],
        out_specs=pl.BlockSpec(memory_space=pltpu.VMEM),
        scratch_shapes=[pltpu.VMEM((CH_DEV, 2, inputs, 2 * SPEC), bf16)],
        compiler_params=pltpu.CompilerParams(vmem_limit_bytes=2**20 * (4 + groups // 4)),
        name="correlate",
    )(gathered)


def solution(mesh):
    placed = (P(("band", "inp"), None), P())
    return jax.shard_map(
        per_device,
        mesh=mesh,
        in_specs=placed,
        out_specs=P(("band", "inp"), None, None, None),
        check_vma=False,
    )
```

```python
import functools
import math

import jax
import jax.numpy as jnp
import numpy as np
from jax import lax
from jax.experimental import pallas as pl
from jax.experimental.pallas import tpu as pltpu
from jax.sharding import PartitionSpec as P

CH_DEV = 2
NFFT = 2048
TAPS = 4
FIRST_CH = 256
SPEC = 128
INP_DEV = 8
FRAMES = SPEC + TAPS - 1
BLOCK = 16
COLS = BLOCK * CH_DEV * 2
HALF = SPEC // 2
HALF_FRAMES = 68
HALF_ROWS = HALF_FRAMES * INP_DEV
LATE_FRAMES = FRAMES - HALF_FRAMES
LOADS = ((0, 32), (32, LATE_FRAMES - 32))
BLOCK_ROWS = CH_DEV * INP_DEV


def dft_table(groups):
    n = np.arange(NFFT, dtype=np.int64)[None, :, None]
    block = np.arange(groups // BLOCK)[:, None, None]
    column = np.arange(2 * COLS)[None, None, :] % COLS
    part = column // BLOCK
    channel = FIRST_CH + (block * BLOCK + column % BLOCK) * CH_DEV + part % CH_DEV
    phase = (n * channel % NFFT).astype(np.float32) * np.float32(2.0 * math.pi / NFFT)
    phase = phase.astype(np.float64)
    table = np.where(part < CH_DEV, np.cos(phase), -np.sin(phase)).astype(np.float32)
    return (table * np.float32(2.0**-19)).astype(jnp.bfloat16)


def for_each(count, body):
    if count == 1:
        body(0)
    else:
        pl.loop(0, count)(body)


def for_each_peer(groups, body):
    if groups <= BLOCK:
        for step in range(1, groups):
            body(step)
    else:
        pl.loop(1, groups)(body)


def kernel(
    groups, samples, taps, table, recv,
    x, taps_v, table_v, weights, prod, volts, turned, send,
    load_sem, sample_sem, own_sem, send_sem, recv_sem,
):
    me = lax.axis_index("inp")
    blocks = groups // BLOCK
    taps_copy = pltpu.make_async_copy(taps, taps_v, load_sem.at[0])
    table_copy = pltpu.make_async_copy(table, table_v, load_sem.at[1])
    taps_copy.start()
    table_copy.start()

    def load(first, count, sem):
        part = pl.ds(first, count)
        return pltpu.make_async_copy(samples.at[part], x.at[part], sem)

    extra = load(LATE_FRAMES, HALF_FRAMES - LATE_FRAMES, load_sem.at[2])
    for h in range(2):
        for index, (first, count) in enumerate(LOADS):
            load(h * HALF_FRAMES + first, count, sample_sem.at[h, index]).start()
        if h == 0:
            extra.start()

    barrier = pltpu.get_barrier_semaphore()

    def greet(step):
        peer = lax.rem(me + step, groups)
        pl.semaphore_signal(
            barrier, inc=1, device_id={"inp": peer}, device_id_type=pl.DeviceIdType.MESH
        )

    for_each_peer(groups, greet)

    width = TAPS * COLS
    tap_of = lax.broadcasted_iota(jnp.int32, (2 * TAPS, width), 1) // COLS
    spread = (tap_of == lax.broadcasted_iota(jnp.int32, (2 * TAPS, width), 0)).astype(jnp.bfloat16)
    taps_copy.wait()
    table_copy.wait()

    tap_rows = taps_v[...].astype(jnp.float32)
    tap_rows = jnp.concatenate([tap_rows, jnp.zeros_like(tap_rows)], axis=0).astype(jnp.bfloat16)
    spread_taps = lax.dot_general(
        tap_rows, spread, (((0,), (0,)), ((), ())), preferred_element_type=jnp.float32
    )

    def weigh(b):
        values = table_v[b].astype(jnp.float32)
        for h in range(2):
            lanes = slice(h * 2 * COLS, (h + 1) * 2 * COLS)
            weights[b, :, lanes] = (values * spread_taps[:, lanes]).astype(jnp.bfloat16)

    for_each(blocks, weigh)

    extra.wait()

    def transfer(peer, source, target):
        return pltpu.make_async_remote_copy(
            src_ref=source,
            dst_ref=target,
            send_sem=send_sem,
            recv_sem=recv_sem,
            device_id={"inp": peer},
            device_id_type=pl.DeviceIdType.MESH,
        )

    def own(h):
        return pltpu.make_async_copy(send.at[me, h], recv.at[me, h], own_sem.at[h])

    @pl.loop(0, 2)
    def _(h):
        for index, (first, count) in enumerate(LOADS):
            load(h * HALF_FRAMES + first, count, sample_sem.at[h, index]).wait()

        def multiply(b):
            rows = pl.ds(pl.multiple_of(h * HALF_ROWS, HALF_ROWS), HALF_ROWS)
            values = x[pl.ds(h * HALF_FRAMES, HALF_FRAMES)].reshape(HALF_ROWS, NFFT)
            prod[b, rows, :] = jnp.dot(values, weights[b], preferred_element_type=jnp.float32)

        for_each(blocks, multiply)

        def turn(b):
            count = HALF * INP_DEV
            start = pl.multiple_of(h * count, count)
            half = (
                prod[b, pl.ds(start, count + INP_DEV), 0:128]
                + prod[b, pl.ds(start + 2 * INP_DEV, count + INP_DEV), 128:256]
            )
            volts[...] = half[:count] + pltpu.roll(half[INP_DEV:], COLS, 1)
            low_lanes = lax.broadcasted_iota(jnp.int32, (HALF, 128), 1) < COLS
            for p in range(2):
                rows = []
                for ia in range(2):
                    i = 4 * ia + 2 * p
                    low = volts[pl.ds(i, HALF, stride=INP_DEV), :]
                    high = volts[pl.ds(i + 1, HALF, stride=INP_DEV), :]
                    rows.append(jnp.where(low_lanes, low, pltpu.roll(high, COLS, 1)))
                pair = jnp.concatenate(rows, axis=0).T
                for k in range(8):
                    to = ((k % 4) * 4 + 2 * p + k // 4) * BLOCK
                    turned[to : to + BLOCK, :] = pair[k * BLOCK : (k + 1) * BLOCK, :]
            first = lax.broadcasted_iota(jnp.int32, (INP_DEV, 128), 1) < HALF
            for g in range(BLOCK):
                real = turned[pl.ds(g, 8, stride=BLOCK), :]
                imag = turned[pl.ds(8 * BLOCK + g, 8, stride=BLOCK), :]
                send[b * BLOCK + g, h] = jnp.concatenate(
                    [
                        jnp.where(first, real, pltpu.roll(imag, HALF, 1)),
                        jnp.where(first, pltpu.roll(real, HALF, 1), imag),
                    ],
                    axis=0,
                ).astype(jnp.bfloat16)

        for_each(blocks, turn)

        @pl.when(h == 0)
        def _():
            pl.semaphore_wait(barrier, groups - 1)

        def start(step):
            peer = lax.rem(me + step, groups)
            transfer(peer, send.at[peer, h], recv.at[me, h]).start()

        for_each_peer(groups, start)

        own(h).start()

    for h in range(2):
        own(h).wait()
    others = pl.ds(0, groups - 1)
    everything = transfer(lax.rem(me + 1, groups), send.at[others], recv.at[others])
    everything.wait_recv()
    everything.wait_send()


def correlate_kernel(recv, out, stack):
    inputs = recv.shape[0] * INP_DEV
    norm = 1.0 / math.sqrt(SPEC)
    shape = (recv.shape[0], INP_DEV, 128)
    upper = lax.broadcasted_iota(jnp.int32, shape, 1) < 4
    first = lax.broadcasted_iota(jnp.int32, (inputs, 128), 1) < HALF
    for h in range(2):
        lanes = slice(h * 128, (h + 1) * 128)
        early = recv[:, h, 0:INP_DEV, :].astype(jnp.float32)
        late = recv[:, h, INP_DEV:, :].astype(jnp.float32)
        by_channel = (
            jnp.where(upper, early, pltpu.roll(late, 4, 1)),
            jnp.where(upper, pltpu.roll(early, 4, 1), late),
        )
        for q in range(CH_DEV):
            values = by_channel[q].reshape(inputs, 128)
            rolled = pltpu.roll(values, HALF, 1)
            stack[q, 0, :, lanes] = values.astype(jnp.bfloat16)
            stack[q, 1, :, lanes] = jnp.where(first, rolled, -rolled).astype(jnp.bfloat16)

    def correlate(tile):
        rows = pl.ds(tile * 128, 128)
        for q in range(CH_DEV):
            for r in range(2):
                product = lax.dot_general(
                    stack[q, r, rows, :], stack[q, 0], (((1,), (1,)), ((), ())),
                    preferred_element_type=jnp.float32,
                )
                out[q, r, rows, :] = (product * norm).astype(jnp.bfloat16)

    for_each(inputs // 128, correlate)


def per_device(samples, taps):
    groups = lax.axis_size("inp")
    blocks = groups // BLOCK
    inputs = groups * INP_DEV
    table = jnp.asarray(dft_table(groups))
    frames = samples.reshape(INP_DEV, FRAMES, NFFT).transpose(1, 0, 2)
    anywhere = pl.BlockSpec(memory_space=pl.ANY)
    bf16, f32 = jnp.bfloat16, jnp.float32
    gathered = pl.pallas_call(
        functools.partial(kernel, groups),
        out_shape=pltpu.VMEM((groups, 2, BLOCK_ROWS, 128), bf16),
        in_specs=[pl.BlockSpec(memory_space=pltpu.HBM)] * 3,
        out_specs=pl.BlockSpec(memory_space=pltpu.VMEM),
        scratch_shapes=[
            pltpu.VMEM((2 * HALF_FRAMES, INP_DEV, NFFT), bf16),
            pltpu.VMEM((TAPS, NFFT), jnp.int32),
            pltpu.VMEM((blocks, NFFT, 2 * COLS), bf16),
            pltpu.VMEM((blocks, NFFT, TAPS * COLS), bf16),
            pltpu.VMEM((blocks, 2 * HALF_ROWS, TAPS * COLS), f32),
            pltpu.VMEM((HALF * INP_DEV, 128), f32),
            pltpu.VMEM((BLOCK_ROWS * BLOCK, 128), f32),
            pltpu.VMEM((groups, 2, BLOCK_ROWS, 128), bf16),
            pltpu.SemaphoreType.DMA((3,)),
            pltpu.SemaphoreType.DMA((2, len(LOADS))),
            pltpu.SemaphoreType.DMA((2,)),
            pltpu.SemaphoreType.DMA,
            pltpu.SemaphoreType.DMA,
        ],
        compiler_params=pltpu.CompilerParams(
            collective_id=0, has_side_effects=True, vmem_limit_bytes=58 * 2**20
        ),
        name="channelize",
    )(frames, taps, table)
    return pl.pallas_call(
        correlate_kernel,
        out_shape=jax.ShapeDtypeStruct((CH_DEV, 2, inputs, inputs), bf16),
        in_specs=[pl.BlockSpec(memory_space=pltpu.VMEM)],
        out_specs=pl.BlockSpec(memory_space=pltpu.VMEM),
        scratch_shapes=[pltpu.VMEM((CH_DEV, 2, inputs, 2 * SPEC), bf16)],
        compiler_params=pltpu.CompilerParams(vmem_limit_bytes=2**20 * (4 + groups // 4)),
        name="correlate",
    )(gathered)


def solution(mesh):
    placed = (P(("band", "inp"), None), P())
    return jax.shard_map(
        per_device,
        mesh=mesh,
        in_specs=placed,
        out_specs=P(("band", "inp"), None, None, None),
        check_vma=False,
    )
```

```python
import functools
import math

import jax
import jax.numpy as jnp
import numpy as np
from jax import lax
from jax.experimental import pallas as pl
from jax.experimental.pallas import tpu as pltpu
from jax.sharding import PartitionSpec as P

CH_DEV = 2
NFFT = 2048
TAPS = 4
FIRST_CH = 256
SPEC = 128
INP_DEV = 8
FRAMES = SPEC + TAPS - 1
BLOCK = 16
COLS = BLOCK * CH_DEV * 2
HALF = SPEC // 2
HALF_FRAMES = 68
HALF_ROWS = HALF_FRAMES * INP_DEV
LATE_FRAMES = FRAMES - HALF_FRAMES
LOADS = ((0, 32), (32, LATE_FRAMES - 32))
BLOCK_ROWS = CH_DEV * INP_DEV


def dft_table(groups):
    n = np.arange(NFFT, dtype=np.int64)[None, :, None]
    block = np.arange(groups // BLOCK)[:, None, None]
    column = np.arange(2 * COLS)[None, None, :] % COLS
    part = column // BLOCK
    channel = FIRST_CH + (block * BLOCK + column % BLOCK) * CH_DEV + part % CH_DEV
    phase = (n * channel % NFFT).astype(np.float32) * np.float32(2.0 * math.pi / NFFT)
    phase = phase.astype(np.float64)
    table = np.where(part < CH_DEV, np.cos(phase), -np.sin(phase)).astype(np.float32)
    return (table * np.float32(2.0**-19)).astype(jnp.bfloat16)


def for_each(count, body):
    if count == 1:
        body(0)
    else:
        pl.loop(0, count)(body)


def for_each_peer(groups, body):
    if groups <= BLOCK:
        for step in range(1, groups):
            body(step)
    else:
        pl.loop(1, groups)(body)


def kernel(
    groups, samples, taps, table, recv,
    x, taps_v, table_v, weights, prod, volts, turned, send,
    load_sem, sample_sem, own_sem, send_sem, recv_sem,
):
    me = lax.axis_index("inp")
    blocks = groups // BLOCK
    taps_copy = pltpu.make_async_copy(taps, taps_v, load_sem.at[0])
    table_copy = pltpu.make_async_copy(table, table_v, load_sem.at[1])
    taps_copy.start()
    table_copy.start()

    def load(first, count, sem):
        part = pl.ds(first, count)
        return pltpu.make_async_copy(samples.at[part], x.at[part], sem)

    extra = load(LATE_FRAMES, HALF_FRAMES - LATE_FRAMES, load_sem.at[2])
    for h in range(2):
        for index, (first, count) in enumerate(LOADS):
            load(h * HALF_FRAMES + first, count, sample_sem.at[h, index]).start()
        if h == 0:
            extra.start()

    barrier = pltpu.get_barrier_semaphore()

    def greet(step):
        peer = lax.rem(me + step, groups)
        pl.semaphore_signal(
            barrier, inc=1, device_id={"inp": peer}, device_id_type=pl.DeviceIdType.MESH
        )

    for_each_peer(groups, greet)

    width = TAPS * COLS
    tap_of = lax.broadcasted_iota(jnp.int32, (2 * TAPS, width), 1) // COLS
    spread = (tap_of == lax.broadcasted_iota(jnp.int32, (2 * TAPS, width), 0)).astype(jnp.bfloat16)
    taps_copy.wait()
    table_copy.wait()

    tap_rows = taps_v[...].astype(jnp.float32)
    tap_rows = jnp.concatenate([tap_rows, jnp.zeros_like(tap_rows)], axis=0).astype(jnp.bfloat16)
    spread_taps = lax.dot_general(
        tap_rows, spread, (((0,), (0,)), ((), ())), preferred_element_type=jnp.float32
    )

    def weigh(b):
        values = table_v[b].astype(jnp.float32)
        for h in range(2):
            lanes = slice(h * 2 * COLS, (h + 1) * 2 * COLS)
            weights[b, :, lanes] = (values * spread_taps[:, lanes]).astype(jnp.bfloat16)

    for_each(blocks, weigh)

    extra.wait()

    def transfer(peer, source, target):
        return pltpu.make_async_remote_copy(
            src_ref=source,
            dst_ref=target,
            send_sem=send_sem,
            recv_sem=recv_sem,
            device_id={"inp": peer},
            device_id_type=pl.DeviceIdType.MESH,
        )

    def own(h):
        return pltpu.make_async_copy(send.at[me, h], recv.at[me, h], own_sem.at[h])

    def multiply_half(h):
        for index, (first, count) in enumerate(LOADS):
            load(h * HALF_FRAMES + first, count, sample_sem.at[h, index]).wait()

        def multiply(b):
            rows = pl.ds(h * HALF_ROWS, HALF_ROWS)
            values = x[pl.ds(h * HALF_FRAMES, HALF_FRAMES)].reshape(HALF_ROWS, NFFT)
            prod[b, rows, :] = jnp.dot(values, weights[b], preferred_element_type=jnp.float32)

        for_each(blocks, multiply)

    def turn_half(h):
        def turn(b):
            count = HALF * INP_DEV
            start = h * count
            half = (
                prod[b, pl.ds(start, count + INP_DEV), 0:128]
                + prod[b, pl.ds(start + 2 * INP_DEV, count + INP_DEV), 128:256]
            )
            volts[...] = half[:count] + pltpu.roll(half[INP_DEV:], COLS, 1)
            low_lanes = lax.broadcasted_iota(jnp.int32, (HALF, 128), 1) < COLS
            for p in range(2):
                rows = []
                for ia in range(2):
                    i = 4 * ia + 2 * p
                    low = volts[pl.ds(i, HALF, stride=INP_DEV), :]
                    high = volts[pl.ds(i + 1, HALF, stride=INP_DEV), :]
                    rows.append(jnp.where(low_lanes, low, pltpu.roll(high, COLS, 1)))
                pair = jnp.concatenate(rows, axis=0).T
                for k in range(8):
                    to = ((k % 4) * 4 + 2 * p + k // 4) * BLOCK
                    turned[to : to + BLOCK, :] = pair[k * BLOCK : (k + 1) * BLOCK, :]
            first = lax.broadcasted_iota(jnp.int32, (INP_DEV, 128), 1) < HALF
            for g in range(BLOCK):
                real = turned[pl.ds(g, 8, stride=BLOCK), :]
                imag = turned[pl.ds(8 * BLOCK + g, 8, stride=BLOCK), :]
                send[b * BLOCK + g, h] = jnp.concatenate(
                    [
                        jnp.where(first, real, pltpu.roll(imag, HALF, 1)),
                        jnp.where(first, pltpu.roll(real, HALF, 1), imag),
                    ],
                    axis=0,
                ).astype(jnp.bfloat16)

        for_each(blocks, turn)

    def send_half(h):
        def start(step):
            peer = lax.rem(me + step, groups)
            transfer(peer, send.at[peer, h], recv.at[me, h]).start()

        for_each_peer(groups, start)
        own(h).start()

    multiply_half(0)
    multiply_half(1)
    turn_half(0)
    pl.semaphore_wait(barrier, groups - 1)
    send_half(0)
    turn_half(1)
    send_half(1)

    for h in range(2):
        own(h).wait()
    others = pl.ds(0, groups - 1)
    everything = transfer(lax.rem(me + 1, groups), send.at[others], recv.at[others])
    everything.wait_recv()
    everything.wait_send()


def correlate_kernel(recv, out, stack, result, out_sem):
    inputs = recv.shape[0] * INP_DEV
    norm = 1.0 / math.sqrt(SPEC)
    shape = (recv.shape[0], INP_DEV, 128)
    upper = lax.broadcasted_iota(jnp.int32, shape, 1) < 4
    first = lax.broadcasted_iota(jnp.int32, (inputs, 128), 1) < HALF
    for h in range(2):
        lanes = slice(h * 128, (h + 1) * 128)
        early = recv[:, h, 0:INP_DEV, :].astype(jnp.float32)
        late = recv[:, h, INP_DEV:, :].astype(jnp.float32)
        by_channel = (
            jnp.where(upper, early, pltpu.roll(late, 4, 1)),
            jnp.where(upper, pltpu.roll(early, 4, 1), late),
        )
        for q in range(CH_DEV):
            values = by_channel[q].reshape(inputs, 128)
            rolled = pltpu.roll(values, HALF, 1)
            stack[q, 0, :, lanes] = values.astype(jnp.bfloat16)
            stack[q, 1, :, lanes] = jnp.where(first, rolled, -rolled).astype(jnp.bfloat16)

    for q in range(CH_DEV):

        def correlate(tile):
            rows = pl.ds(tile * 128, 128)
            left = jnp.concatenate([stack[q, 0, rows, :], stack[q, 1, rows, :]], axis=0)
            product = lax.dot_general(
                left, stack[q, 0], (((1,), (1,)), ((), ())), preferred_element_type=jnp.float32
            )
            product = (product * norm).astype(jnp.bfloat16)
            result[q, 0, rows, :] = product[:128]
            result[q, 1, rows, :] = product[128:]

        for_each(inputs // 128, correlate)
        pltpu.make_async_copy(result.at[q], out.at[q], out_sem.at[q]).start()
    for q in range(CH_DEV):
        pltpu.make_async_copy(result.at[q], out.at[q], out_sem.at[q]).wait()


def per_device(samples, taps):
    groups = lax.axis_size("inp")
    blocks = groups // BLOCK
    inputs = groups * INP_DEV
    table = jnp.asarray(dft_table(groups))
    frames = samples.reshape(INP_DEV, FRAMES, NFFT).transpose(1, 0, 2)
    anywhere = pl.BlockSpec(memory_space=pl.ANY)
    bf16, f32 = jnp.bfloat16, jnp.float32
    gathered = pl.pallas_call(
        functools.partial(kernel, groups),
        out_shape=pltpu.VMEM((groups, 2, BLOCK_ROWS, 128), bf16),
        in_specs=[pl.BlockSpec(memory_space=pltpu.HBM)] * 3,
        out_specs=pl.BlockSpec(memory_space=pltpu.VMEM),
        scratch_shapes=[
            pltpu.VMEM((2 * HALF_FRAMES, INP_DEV, NFFT), bf16),
            pltpu.VMEM((TAPS, NFFT), jnp.int32),
            pltpu.VMEM((blocks, NFFT, 2 * COLS), bf16),
            pltpu.VMEM((blocks, NFFT, TAPS * COLS), bf16),
            pltpu.VMEM((blocks, 2 * HALF_ROWS, TAPS * COLS), f32),
            pltpu.VMEM((HALF * INP_DEV, 128), f32),
            pltpu.VMEM((BLOCK_ROWS * BLOCK, 128), f32),
            pltpu.VMEM((groups, 2, BLOCK_ROWS, 128), bf16),
            pltpu.SemaphoreType.DMA((3,)),
            pltpu.SemaphoreType.DMA((2, len(LOADS))),
            pltpu.SemaphoreType.DMA((2,)),
            pltpu.SemaphoreType.DMA,
            pltpu.SemaphoreType.DMA,
        ],
        compiler_params=pltpu.CompilerParams(
            collective_id=0, has_side_effects=True, vmem_limit_bytes=58 * 2**20
        ),
        name="channelize",
    )(frames, taps, table)
    return pl.pallas_call(
        correlate_kernel,
        out_shape=jax.ShapeDtypeStruct((CH_DEV, 2, inputs, inputs), bf16),
        in_specs=[pl.BlockSpec(memory_space=pltpu.VMEM)],
        out_specs=anywhere,
        scratch_shapes=[
            pltpu.VMEM((CH_DEV, 2, inputs, 2 * SPEC), bf16),
            pltpu.VMEM((CH_DEV, 2, inputs, inputs), bf16),
            pltpu.SemaphoreType.DMA((CH_DEV,)),
        ],
        compiler_params=pltpu.CompilerParams(vmem_limit_bytes=2**20 * (4 + groups // 4)),
        name="correlate",
    )(gathered)


def solution(mesh):
    placed = (P(("band", "inp"), None), P())
    return jax.shard_map(
        per_device,
        mesh=mesh,
        in_specs=placed,
        out_specs=P(("band", "inp"), None, None, None),
        check_vma=False,
    )
```

```python
import functools
import math

import jax
import jax.numpy as jnp
import numpy as np
from jax import lax
from jax.experimental import pallas as pl
from jax.experimental.pallas import tpu as pltpu
from jax.sharding import PartitionSpec as P

CH_DEV = 2
NFFT = 2048
TAPS = 4
FIRST_CH = 256
SPEC = 128
INP_DEV = 8
FRAMES = SPEC + TAPS - 1
BLOCK = 16
COLS = BLOCK * CH_DEV * 2
HALF = SPEC // 2
HALF_FRAMES = 68
HALF_ROWS = HALF_FRAMES * INP_DEV
LATE_FRAMES = FRAMES - HALF_FRAMES
LOADS = ((0, 32), (32, LATE_FRAMES - 32))
BLOCK_ROWS = CH_DEV * INP_DEV


def dft_table(groups):
    n = np.arange(NFFT, dtype=np.int64)[None, :, None]
    block = np.arange(groups // BLOCK)[:, None, None]
    column = np.arange(2 * COLS)[None, None, :] % COLS
    part = column // BLOCK
    channel = FIRST_CH + (block * BLOCK + column % BLOCK) * CH_DEV + part % CH_DEV
    phase = (n * channel % NFFT).astype(np.float32) * np.float32(2.0 * math.pi / NFFT)
    phase = phase.astype(np.float64)
    table = np.where(part < CH_DEV, np.cos(phase), -np.sin(phase)).astype(np.float32)
    return (table * np.float32(2.0**-19)).astype(jnp.bfloat16)


def for_each(count, body):
    if count == 1:
        body(0)
    else:
        pl.loop(0, count)(body)


def for_each_peer(groups, body):
    if groups <= BLOCK:
        for step in range(1, groups):
            body(step)
    else:
        pl.loop(1, groups)(body)


def kernel(
    groups, samples, taps, table, recv,
    x, taps_v, table_v, weights, prod, volts, turned, send,
    load_sem, sample_sem, own_sem, send_sem, recv_sem,
):
    me = lax.axis_index("inp")
    blocks = groups // BLOCK
    taps_copy = pltpu.make_async_copy(taps, taps_v, load_sem.at[0])
    table_copy = pltpu.make_async_copy(table, table_v, load_sem.at[1])
    taps_copy.start()
    table_copy.start()

    def load(first, count, sem):
        part = pl.ds(first, count)
        return pltpu.make_async_copy(samples.at[part], x.at[part], sem)

    extra = load(LATE_FRAMES, HALF_FRAMES - LATE_FRAMES, load_sem.at[2])
    for h in range(2):
        for index, (first, count) in enumerate(LOADS):
            load(h * HALF_FRAMES + first, count, sample_sem.at[h, index]).start()
        if h == 0:
            extra.start()

    barrier = pltpu.get_barrier_semaphore()

    def greet(step):
        peer = lax.rem(me + step, groups)
        pl.semaphore_signal(
            barrier, inc=1, device_id={"inp": peer}, device_id_type=pl.DeviceIdType.MESH
        )

    for_each_peer(groups, greet)

    width = TAPS * COLS
    tap_of = lax.broadcasted_iota(jnp.int32, (2 * TAPS, width), 1) // COLS
    spread = (tap_of == lax.broadcasted_iota(jnp.int32, (2 * TAPS, width), 0)).astype(jnp.bfloat16)
    taps_copy.wait()
    table_copy.wait()

    tap_rows = taps_v[...].astype(jnp.float32)
    tap_rows = jnp.concatenate([tap_rows, jnp.zeros_like(tap_rows)], axis=0).astype(jnp.bfloat16)
    spread_taps = lax.dot_general(
        tap_rows, spread, (((0,), (0,)), ((), ())), preferred_element_type=jnp.float32
    )

    def weigh(b):
        for h in range(2):
            lanes = slice(h * 2 * COLS, (h + 1) * 2 * COLS)
            weights[b, :, lanes] = table_v[b] * spread_taps[:, lanes].astype(jnp.bfloat16)

    for_each(blocks, weigh)

    extra.wait()

    def transfer(peer, source, target):
        return pltpu.make_async_remote_copy(
            src_ref=source,
            dst_ref=target,
            send_sem=send_sem,
            recv_sem=recv_sem,
            device_id={"inp": peer},
            device_id_type=pl.DeviceIdType.MESH,
        )

    def own(h):
        return pltpu.make_async_copy(send.at[me, h], recv.at[me, h], own_sem.at[h])

    @pl.loop(0, 2)
    def _(h):
        for index, (first, count) in enumerate(LOADS):
            load(h * HALF_FRAMES + first, count, sample_sem.at[h, index]).wait()

        def multiply(b):
            step = HALF_FRAMES // 2

            @pl.loop(0, HALF_FRAMES // step)
            def _(tile):
                first = h * HALF_FRAMES + tile * step
                values = x[pl.ds(first, step)].reshape(step * INP_DEV, NFFT)
                rows = pl.ds(pl.multiple_of(first * INP_DEV, INP_DEV), step * INP_DEV)
                prod[b, rows, :] = jnp.dot(values, weights[b], preferred_element_type=jnp.float32)

        for_each(blocks, multiply)

        def turn(b):
            count = HALF * INP_DEV
            start = pl.multiple_of(h * count, count)
            half = (
                prod[b, pl.ds(start, count + INP_DEV), 0:128]
                + prod[b, pl.ds(start + 2 * INP_DEV, count + INP_DEV), 128:256]
            )
            volts[...] = half[:count] + pltpu.roll(half[INP_DEV:], COLS, 1)
            low_lanes = lax.broadcasted_iota(jnp.int32, (HALF, 128), 1) < COLS
            for p in range(2):
                rows = []
                for ia in range(2):
                    i = 4 * ia + 2 * p
                    low = volts[pl.ds(i, HALF, stride=INP_DEV), :]
                    high = volts[pl.ds(i + 1, HALF, stride=INP_DEV), :]
                    rows.append(jnp.where(low_lanes, low, pltpu.roll(high, COLS, 1)))
                pair = jnp.concatenate(rows, axis=0).T
                for k in range(8):
                    to = ((k % 4) * 4 + 2 * p + k // 4) * BLOCK
                    turned[to : to + BLOCK, :] = pair[k * BLOCK : (k + 1) * BLOCK, :]
            first = lax.broadcasted_iota(jnp.int32, (INP_DEV, 128), 1) < HALF
            @pl.loop(0, BLOCK, unroll=4)
            def _(g):
                real = turned[pl.ds(g, 8, stride=BLOCK), :]
                imag = turned[pl.ds(8 * BLOCK + g, 8, stride=BLOCK), :]
                send[b * BLOCK + g, h] = jnp.concatenate(
                    [
                        jnp.where(first, real, pltpu.roll(imag, HALF, 1)),
                        jnp.where(first, pltpu.roll(real, HALF, 1), imag),
                    ],
                    axis=0,
                ).astype(jnp.bfloat16)

        for_each(blocks, turn)

        @pl.when(h == 0)
        def _():
            pl.semaphore_wait(barrier, groups - 1)

        def start(step):
            peer = lax.rem(me + step, groups)
            transfer(peer, send.at[peer, h], recv.at[me, h]).start()

        for_each_peer(groups, start)

        own(h).start()

    for h in range(2):
        own(h).wait()
    others = pl.ds(0, groups - 1)
    everything = transfer(lax.rem(me + 1, groups), send.at[others], recv.at[others])
    everything.wait_recv()
    everything.wait_send()


def correlate_kernel(recv, out, stack):
    inputs = recv.shape[0] * INP_DEV
    norm = 1.0 / math.sqrt(SPEC)
    shape = (recv.shape[0], INP_DEV, 128)
    upper = lax.broadcasted_iota(jnp.int32, shape, 1) < 4
    first = lax.broadcasted_iota(jnp.int32, (inputs, 128), 1) < HALF
    for h in range(2):
        lanes = slice(h * 128, (h + 1) * 128)
        early = recv[:, h, 0:INP_DEV, :].astype(jnp.float32)
        late = recv[:, h, INP_DEV:, :].astype(jnp.float32)
        by_channel = (
            jnp.where(upper, early, pltpu.roll(late, 4, 1)),
            jnp.where(upper, pltpu.roll(early, 4, 1), late),
        )
        for q in range(CH_DEV):
            values = by_channel[q].reshape(inputs, 128)
            rolled = pltpu.roll(values, HALF, 1)
            stack[q, 0, :, lanes] = values.astype(jnp.bfloat16)
            stack[q, 1, :, lanes] = jnp.where(first, rolled, -rolled).astype(jnp.bfloat16)

    def correlate(tile):
        rows = pl.ds(tile * 128, 128)
        for q in range(CH_DEV):
            for r in range(2):
                product = lax.dot_general(
                    stack[q, r, rows, :], stack[q, 0], (((1,), (1,)), ((), ())),
                    preferred_element_type=jnp.float32,
                )
                out[q, r, rows, :] = (product * norm).astype(jnp.bfloat16)

    for_each(inputs // 128, correlate)


def per_device(samples, taps):
    groups = lax.axis_size("inp")
    blocks = groups // BLOCK
    inputs = groups * INP_DEV
    table = jnp.asarray(dft_table(groups))
    frames = samples.reshape(INP_DEV, FRAMES, NFFT).transpose(1, 0, 2)
    anywhere = pl.BlockSpec(memory_space=pl.ANY)
    bf16, f32 = jnp.bfloat16, jnp.float32
    gathered = pl.pallas_call(
        functools.partial(kernel, groups),
        out_shape=pltpu.VMEM((groups, 2, BLOCK_ROWS, 128), bf16),
        in_specs=[pl.BlockSpec(memory_space=pltpu.HBM)] * 3,
        out_specs=pl.BlockSpec(memory_space=pltpu.VMEM),
        scratch_shapes=[
            pltpu.VMEM((2 * HALF_FRAMES, INP_DEV, NFFT), bf16),
            pltpu.VMEM((TAPS, NFFT), jnp.int32),
            pltpu.VMEM((blocks, NFFT, 2 * COLS), bf16),
            pltpu.VMEM((blocks, NFFT, TAPS * COLS), bf16),
            pltpu.VMEM((blocks, 2 * HALF_ROWS, TAPS * COLS), f32),
            pltpu.VMEM((HALF * INP_DEV, 128), f32),
            pltpu.VMEM((BLOCK_ROWS * BLOCK, 128), f32),
            pltpu.VMEM((groups, 2, BLOCK_ROWS, 128), bf16),
            pltpu.SemaphoreType.DMA((3,)),
            pltpu.SemaphoreType.DMA((2, len(LOADS))),
            pltpu.SemaphoreType.DMA((2,)),
            pltpu.SemaphoreType.DMA,
            pltpu.SemaphoreType.DMA,
        ],
        compiler_params=pltpu.CompilerParams(
            collective_id=0, has_side_effects=True, vmem_limit_bytes=58 * 2**20
        ),
        name="channelize",
    )(frames, taps, table)
    return pl.pallas_call(
        correlate_kernel,
        out_shape=jax.ShapeDtypeStruct((CH_DEV, 2, inputs, inputs), bf16),
        in_specs=[pl.BlockSpec(memory_space=pltpu.VMEM)],
        out_specs=pl.BlockSpec(memory_space=pltpu.VMEM),
        scratch_shapes=[pltpu.VMEM((CH_DEV, 2, inputs, 2 * SPEC), bf16)],
        compiler_params=pltpu.CompilerParams(vmem_limit_bytes=2**20 * (4 + groups // 4)),
        name="correlate",
    )(gathered)


def solution(mesh):
    placed = (P(("band", "inp"), None), P())
    return jax.shard_map(
        per_device,
        mesh=mesh,
        in_specs=placed,
        out_specs=P(("band", "inp"), None, None, None),
        check_vma=False,
    )
```

```python
import functools
import math

import jax
import jax.numpy as jnp
import numpy as np
from jax import lax
from jax.experimental import pallas as pl
from jax.experimental.pallas import tpu as pltpu
from jax.sharding import PartitionSpec as P

CH_DEV = 2
NFFT = 2048
TAPS = 4
FIRST_CH = 256
SPEC = 128
INP_DEV = 8
FRAMES = SPEC + TAPS - 1
BLOCK = 16
COLS = BLOCK * CH_DEV * 2
HALF = SPEC // 2
HALF_FRAMES = 68
HALF_ROWS = HALF_FRAMES * INP_DEV
LATE_FRAMES = FRAMES - HALF_FRAMES
BLOCK_ROWS = CH_DEV * INP_DEV


def dft_table(groups):
    n = np.arange(NFFT, dtype=np.int64)[None, :, None]
    block = np.arange(groups // BLOCK)[:, None, None]
    column = np.arange(2 * COLS)[None, None, :] % COLS
    part = column // BLOCK
    channel = FIRST_CH + (block * BLOCK + column % BLOCK) * CH_DEV + part % CH_DEV
    phase = (n * channel % NFFT).astype(np.float32) * np.float32(2.0 * math.pi / NFFT)
    phase = phase.astype(np.float64)
    table = np.where(part < CH_DEV, np.cos(phase), -np.sin(phase)).astype(np.float32)
    return (table * np.float32(2.0**-19)).astype(jnp.bfloat16)


def for_each(count, body):
    if count == 1:
        body(0)
    else:
        pl.loop(0, count)(body)


def for_each_peer(groups, body):
    if groups <= BLOCK:
        for step in range(1, groups):
            body(step)
    else:
        pl.loop(1, groups)(body)


def kernel(
    groups, samples, taps, table, recv,
    x, taps_v, table_v, weights, prod, volts, turned, send,
    load_sem, sample_sem, own_sem, send_sem, recv_sem,
):
    me = lax.axis_index("inp")
    blocks = groups // BLOCK
    taps_copy = pltpu.make_async_copy(taps, taps_v, load_sem.at[0])
    table_copy = pltpu.make_async_copy(table, table_v, load_sem.at[1])
    taps_copy.start()
    table_copy.start()

    def load(h, part):
        frames = pl.ds(h * HALF_FRAMES, (HALF_FRAMES, LATE_FRAMES)[h])
        span = pl.ds(part * (NFFT // 2), NFFT // 2)
        return pltpu.make_async_copy(
            samples.at[frames, :, span], x.at[frames, :, span], sample_sem.at[h, part]
        )

    for h in range(2):
        for part in range(2):
            load(h, part).start()

    barrier = pltpu.get_barrier_semaphore()

    def greet(step):
        peer = lax.rem(me + step, groups)
        pl.semaphore_signal(
            barrier, inc=1, device_id={"inp": peer}, device_id_type=pl.DeviceIdType.MESH
        )

    for_each_peer(groups, greet)

    width = TAPS * COLS
    tap_of = lax.broadcasted_iota(jnp.int32, (2 * TAPS, width), 1) // COLS
    spread = (tap_of == lax.broadcasted_iota(jnp.int32, (2 * TAPS, width), 0)).astype(jnp.bfloat16)
    taps_copy.wait()
    table_copy.wait()

    depth = NFFT // 2

    def weigh_part(part):
        rows = slice(part * depth, (part + 1) * depth)
        tap_rows = taps_v[:, rows].astype(jnp.float32)
        tap_rows = jnp.concatenate([tap_rows, jnp.zeros_like(tap_rows)], axis=0)
        spread_taps = lax.dot_general(
            tap_rows.astype(jnp.bfloat16), spread, (((0,), (0,)), ((), ())),
            preferred_element_type=jnp.float32,
        ).astype(jnp.bfloat16)

        def weigh(b):
            for h in range(2):
                lanes = slice(h * 2 * COLS, (h + 1) * 2 * COLS)
                weights[b, rows, lanes] = table_v[b, rows, :] * spread_taps[:, lanes]

        for_each(blocks, weigh)

    def transfer(peer, source, target):
        return pltpu.make_async_remote_copy(
            src_ref=source,
            dst_ref=target,
            send_sem=send_sem,
            recv_sem=recv_sem,
            device_id={"inp": peer},
            device_id_type=pl.DeviceIdType.MESH,
        )

    def own(h):
        return pltpu.make_async_copy(send.at[me, h], recv.at[me, h], own_sem.at[h])

    def multiply_part(h, part):
        def multiply(b):
            rows = pl.ds(h * HALF_ROWS, HALF_ROWS)
            span = slice(part * depth, (part + 1) * depth)
            values = x[pl.ds(h * HALF_FRAMES, HALF_FRAMES), :, span].reshape(HALF_ROWS, depth)
            product = jnp.dot(values, weights[b, span, :], preferred_element_type=jnp.float32)
            if part == 0:
                prod[b, rows, :] = product
            else:
                prod[b, rows, :] += product

        for_each(blocks, multiply)

    def turn_half(h):
        def turn(b):
            count = HALF * INP_DEV
            start = h * count
            half = (
                prod[b, pl.ds(start, count + INP_DEV), 0:128]
                + prod[b, pl.ds(start + 2 * INP_DEV, count + INP_DEV), 128:256]
            )
            volts[...] = half[:count] + pltpu.roll(half[INP_DEV:], COLS, 1)
            low_lanes = lax.broadcasted_iota(jnp.int32, (HALF, 128), 1) < COLS
            for p in range(2):
                rows = []
                for ia in range(2):
                    i = 4 * ia + 2 * p
                    low = volts[pl.ds(i, HALF, stride=INP_DEV), :]
                    high = volts[pl.ds(i + 1, HALF, stride=INP_DEV), :]
                    rows.append(jnp.where(low_lanes, low, pltpu.roll(high, COLS, 1)))
                pair = jnp.concatenate(rows, axis=0).T
                for k in range(8):
                    to = ((k % 4) * 4 + 2 * p + k // 4) * BLOCK
                    turned[to : to + BLOCK, :] = pair[k * BLOCK : (k + 1) * BLOCK, :]
            first = lax.broadcasted_iota(jnp.int32, (INP_DEV, 128), 1) < HALF
            for g in range(BLOCK):
                real = turned[pl.ds(g, 8, stride=BLOCK), :]
                imag = turned[pl.ds(8 * BLOCK + g, 8, stride=BLOCK), :]
                send[b * BLOCK + g, h] = jnp.concatenate(
                    [
                        jnp.where(first, real, pltpu.roll(imag, HALF, 1)),
                        jnp.where(first, pltpu.roll(real, HALF, 1), imag),
                    ],
                    axis=0,
                ).astype(jnp.bfloat16)

        for_each(blocks, turn)

    def send_half(h):
        def start(step):
            peer = lax.rem(me + step, groups)
            transfer(peer, send.at[peer, h], recv.at[me, h]).start()

        for_each_peer(groups, start)
        own(h).start()

    weigh_part(0)
    load(0, 0).wait()
    multiply_part(0, 0)
    weigh_part(1)
    load(0, 1).wait()
    multiply_part(0, 1)
    load(1, 0).wait()
    multiply_part(1, 0)
    turn_half(0)
    pl.semaphore_wait(barrier, groups - 1)
    send_half(0)
    load(1, 1).wait()
    multiply_part(1, 1)
    turn_half(1)
    send_half(1)

    for h in range(2):
        own(h).wait()
    others = pl.ds(0, groups - 1)
    everything = transfer(lax.rem(me + 1, groups), send.at[others], recv.at[others])
    everything.wait_recv()
    everything.wait_send()


def correlate_kernel(recv, out, stack, result, out_sem):
    inputs = recv.shape[0] * INP_DEV
    norm = 1.0 / math.sqrt(SPEC)
    shape = (recv.shape[0], INP_DEV, 128)
    upper = lax.broadcasted_iota(jnp.int32, shape, 1) < 4
    first = lax.broadcasted_iota(jnp.int32, (inputs, 128), 1) < HALF
    for h in range(2):
        lanes = slice(h * 128, (h + 1) * 128)
        early = recv[:, h, 0:INP_DEV, :].astype(jnp.float32)
        late = recv[:, h, INP_DEV:, :].astype(jnp.float32)
        by_channel = (
            jnp.where(upper, early, pltpu.roll(late, 4, 1)),
            jnp.where(upper, pltpu.roll(early, 4, 1), late),
        )
        for q in range(CH_DEV):
            values = by_channel[q].reshape(inputs, 128)
            rolled = pltpu.roll(values, HALF, 1)
            stack[q, 0, :, lanes] = values.astype(jnp.bfloat16)
            stack[q, 1, :, lanes] = jnp.where(first, rolled, -rolled).astype(jnp.bfloat16)

    for q in range(CH_DEV):

        def correlate(tile):
            rows = pl.ds(tile * 128, 128)
            left = jnp.concatenate([stack[q, 0, rows, :], stack[q, 1, rows, :]], axis=0)
            product = lax.dot_general(
                left, stack[q, 0], (((1,), (1,)), ((), ())), preferred_element_type=jnp.float32
            )
            product = (product * norm).astype(jnp.bfloat16)
            result[q, 0, rows, :] = product[:128]
            result[q, 1, rows, :] = product[128:]

        for_each(inputs // 128, correlate)
        pltpu.make_async_copy(result.at[q], out.at[q], out_sem.at[q]).start()
    for q in range(CH_DEV):
        pltpu.make_async_copy(result.at[q], out.at[q], out_sem.at[q]).wait()


def per_device(samples, taps):
    groups = lax.axis_size("inp")
    blocks = groups // BLOCK
    inputs = groups * INP_DEV
    table = jnp.asarray(dft_table(groups))
    frames = samples.reshape(INP_DEV, FRAMES, NFFT).transpose(1, 0, 2)
    anywhere = pl.BlockSpec(memory_space=pl.ANY)
    bf16, f32 = jnp.bfloat16, jnp.float32
    gathered = pl.pallas_call(
        functools.partial(kernel, groups),
        out_shape=pltpu.VMEM((groups, 2, BLOCK_ROWS, 128), bf16),
        in_specs=[pl.BlockSpec(memory_space=pltpu.HBM)] * 3,
        out_specs=pl.BlockSpec(memory_space=pltpu.VMEM),
        scratch_shapes=[
            pltpu.VMEM((2 * HALF_FRAMES, INP_DEV, NFFT), bf16),
            pltpu.VMEM((TAPS, NFFT), jnp.int32),
            pltpu.VMEM((blocks, NFFT, 2 * COLS), bf16),
            pltpu.VMEM((blocks, NFFT, TAPS * COLS), bf16),
            pltpu.VMEM((blocks, 2 * HALF_ROWS, TAPS * COLS), f32),
            pltpu.VMEM((HALF * INP_DEV, 128), f32),
            pltpu.VMEM((BLOCK_ROWS * BLOCK, 128), f32),
            pltpu.VMEM((groups, 2, BLOCK_ROWS, 128), bf16),
            pltpu.SemaphoreType.DMA((2,)),
            pltpu.SemaphoreType.DMA((2, 2)),
            pltpu.SemaphoreType.DMA((2,)),
            pltpu.SemaphoreType.DMA,
            pltpu.SemaphoreType.DMA,
        ],
        compiler_params=pltpu.CompilerParams(
            collective_id=0, has_side_effects=True, vmem_limit_bytes=58 * 2**20
        ),
        name="channelize",
    )(frames, taps, table)
    return pl.pallas_call(
        correlate_kernel,
        out_shape=jax.ShapeDtypeStruct((CH_DEV, 2, inputs, inputs), bf16),
        in_specs=[pl.BlockSpec(memory_space=pltpu.VMEM)],
        out_specs=anywhere,
        scratch_shapes=[
            pltpu.VMEM((CH_DEV, 2, inputs, 2 * SPEC), bf16),
            pltpu.VMEM((CH_DEV, 2, inputs, inputs), bf16),
            pltpu.SemaphoreType.DMA((CH_DEV,)),
        ],
        compiler_params=pltpu.CompilerParams(vmem_limit_bytes=2**20 * (4 + groups // 4)),
        name="correlate",
    )(gathered)


def solution(mesh):
    placed = (P(("band", "inp"), None), P())
    return jax.shard_map(
        per_device,
        mesh=mesh,
        in_specs=placed,
        out_specs=P(("band", "inp"), None, None, None),
        check_vma=False,
    )
```

```python
import functools
import math

import jax
import jax.numpy as jnp
import numpy as np
from jax import lax
from jax.experimental import pallas as pl
from jax.experimental.pallas import tpu as pltpu
from jax.sharding import PartitionSpec as P

CH_DEV = 2
NFFT = 2048
TAPS = 4
FIRST_CH = 256
SPEC = 128
INP_DEV = 8
FRAMES = SPEC + TAPS - 1
BLOCK = 16
COLS = BLOCK * CH_DEV * 2
HALF = SPEC // 2
HALF_FRAMES = 68
HALF_ROWS = HALF_FRAMES * INP_DEV
LATE_FRAMES = FRAMES - HALF_FRAMES
LOADS = ((0, 32), (32, LATE_FRAMES - 32))
BLOCK_ROWS = CH_DEV * INP_DEV


def dft_table(groups):
    n = np.arange(NFFT, dtype=np.int64)[None, :, None]
    block = np.arange(groups // BLOCK)[:, None, None]
    column = np.arange(2 * COLS)[None, None, :] % COLS
    part = column // BLOCK
    channel = FIRST_CH + (block * BLOCK + column % BLOCK) * CH_DEV + part % CH_DEV
    phase = (n * channel % NFFT).astype(np.float32) * np.float32(2.0 * math.pi / NFFT)
    phase = phase.astype(np.float64)
    table = np.where(part < CH_DEV, np.cos(phase), -np.sin(phase)).astype(np.float32)
    return (table * np.float32(2.0**-19)).astype(jnp.bfloat16)


def for_each(count, body):
    if count == 1:
        body(0)
    else:
        pl.loop(0, count)(body)


def for_each_peer(groups, body):
    pl.loop(1, groups, unroll=3 if groups <= BLOCK else 1)(body)


def kernel(
    groups, samples, taps, table, recv,
    x, taps_v, table_v, weights, prod, volts, turned, send,
    load_sem, sample_sem, own_sem, send_sem, recv_sem,
):
    me = lax.axis_index("inp")
    blocks = groups // BLOCK
    taps_copy = pltpu.make_async_copy(taps, taps_v, load_sem.at[0])
    table_copy = pltpu.make_async_copy(table, table_v, load_sem.at[1])
    taps_copy.start()
    table_copy.start()

    def load(first, count, sem):
        part = pl.ds(first, count)
        return pltpu.make_async_copy(samples.at[part], x.at[part], sem)

    extra = load(LATE_FRAMES, HALF_FRAMES - LATE_FRAMES, load_sem.at[2])
    for h in range(2):
        for index, (first, count) in enumerate(LOADS):
            load(h * HALF_FRAMES + first, count, sample_sem.at[h, index]).start()
        if h == 0:
            extra.start()

    barrier = pltpu.get_barrier_semaphore()

    def greet(step):
        peer = lax.rem(me + step, groups)
        pl.semaphore_signal(
            barrier, inc=1, device_id={"inp": peer}, device_id_type=pl.DeviceIdType.MESH
        )

    for_each_peer(groups, greet)

    width = TAPS * COLS
    tap_of = lax.broadcasted_iota(jnp.int32, (2 * TAPS, width), 1) // COLS
    spread = (tap_of == lax.broadcasted_iota(jnp.int32, (2 * TAPS, width), 0)).astype(jnp.bfloat16)
    taps_copy.wait()
    table_copy.wait()

    depth = NFFT // 4

    @pl.loop(0, NFFT // depth)
    def _(tile):
        rows = pl.ds(pl.multiple_of(tile * depth, depth), depth)
        tap_rows = taps_v[:, rows].astype(jnp.float32)
        tap_rows = jnp.concatenate([tap_rows, jnp.zeros_like(tap_rows)], axis=0)
        spread_taps = lax.dot_general(
            tap_rows.astype(jnp.bfloat16), spread, (((0,), (0,)), ((), ())),
            preferred_element_type=jnp.float32,
        ).astype(jnp.bfloat16)

        def weigh(b):
            for h in range(2):
                lanes = slice(h * 2 * COLS, (h + 1) * 2 * COLS)
                weights[b, rows, lanes] = table_v[b, rows, :] * spread_taps[:, lanes]

        for_each(blocks, weigh)

    extra.wait()

    def transfer(peer, source, target):
        return pltpu.make_async_remote_copy(
            src_ref=source,
            dst_ref=target,
            send_sem=send_sem,
            recv_sem=recv_sem,
            device_id={"inp": peer},
            device_id_type=pl.DeviceIdType.MESH,
        )

    def own(h):
        return pltpu.make_async_copy(send.at[me, h], recv.at[me, h], own_sem.at[h])

    @pl.loop(0, 2)
    def _(h):
        for index, (first, count) in enumerate(LOADS):
            load(h * HALF_FRAMES + first, count, sample_sem.at[h, index]).wait()

        def multiply(b):
            rows = pl.ds(pl.multiple_of(h * HALF_ROWS, HALF_ROWS), HALF_ROWS)
            values = x[pl.ds(h * HALF_FRAMES, HALF_FRAMES)].reshape(HALF_ROWS, NFFT)
            prod[b, rows, :] = jnp.dot(values, weights[b], preferred_element_type=jnp.float32)

        for_each(blocks, multiply)

        def turn(b):
            count = HALF * INP_DEV
            start = pl.multiple_of(h * count, count)
            half = (
                prod[b, pl.ds(start, count + INP_DEV), 0:128]
                + prod[b, pl.ds(start + 2 * INP_DEV, count + INP_DEV), 128:256]
            )
            volts[...] = half[:count] + pltpu.roll(half[INP_DEV:], COLS, 1)
            low_lanes = lax.broadcasted_iota(jnp.int32, (HALF, 128), 1) < COLS
            for p in range(2):
                rows = []
                for ia in range(2):
                    i = 4 * ia + 2 * p
                    low = volts[pl.ds(i, HALF, stride=INP_DEV), :]
                    high = volts[pl.ds(i + 1, HALF, stride=INP_DEV), :]
                    rows.append(jnp.where(low_lanes, low, pltpu.roll(high, COLS, 1)))
                pair = jnp.concatenate(rows, axis=0).T
                for k in range(8):
                    to = ((k % 4) * 4 + 2 * p + k // 4) * BLOCK
                    turned[to : to + BLOCK, :] = pair[k * BLOCK : (k + 1) * BLOCK, :]
            first = lax.broadcasted_iota(jnp.int32, (INP_DEV, 128), 1) < HALF
            @pl.loop(0, BLOCK, unroll=4)
            def _(g):
                real = turned[pl.ds(g, 8, stride=BLOCK), :]
                imag = turned[pl.ds(8 * BLOCK + g, 8, stride=BLOCK), :]
                send[b * BLOCK + g, h] = jnp.concatenate(
                    [
                        jnp.where(first, real, pltpu.roll(imag, HALF, 1)),
                        jnp.where(first, pltpu.roll(real, HALF, 1), imag),
                    ],
                    axis=0,
                ).astype(jnp.bfloat16)

        for_each(blocks, turn)

        @pl.when(h == 0)
        def _():
            pl.semaphore_wait(barrier, groups - 1)

        def start(step):
            peer = lax.rem(me + step, groups)
            transfer(peer, send.at[peer, h], recv.at[me, h]).start()

        for_each_peer(groups, start)

        own(h).start()

    for h in range(2):
        own(h).wait()
    others = pl.ds(0, groups - 1)
    everything = transfer(lax.rem(me + 1, groups), send.at[others], recv.at[others])
    everything.wait_recv()
    everything.wait_send()


def correlate_kernel(recv, out, stack):
    inputs = recv.shape[0] * INP_DEV
    norm = 1.0 / math.sqrt(SPEC)
    shape = (recv.shape[0], INP_DEV, 128)
    upper = lax.broadcasted_iota(jnp.int32, shape, 1) < 4
    first = lax.broadcasted_iota(jnp.int32, (inputs, 128), 1) < HALF
    @pl.loop(0, 2)
    def _(h):
        lanes = pl.ds(pl.multiple_of(h * 128, 128), 128)
        early = recv[:, h, 0:INP_DEV, :].astype(jnp.float32)
        late = recv[:, h, INP_DEV:, :].astype(jnp.float32)
        by_channel = (
            jnp.where(upper, early, pltpu.roll(late, 4, 1)),
            jnp.where(upper, pltpu.roll(early, 4, 1), late),
        )
        for q in range(CH_DEV):
            values = by_channel[q].reshape(inputs, 128)
            rolled = pltpu.roll(values, HALF, 1)
            stack[q, 0, :, lanes] = values.astype(jnp.bfloat16)
            stack[q, 1, :, lanes] = jnp.where(first, rolled, -rolled).astype(jnp.bfloat16)

    def correlate(tile):
        rows = pl.ds(tile * 128, 128)

        @pl.loop(0, CH_DEV)
        def _(q):
            left = jnp.concatenate([stack[q, 0, rows, :], stack[q, 1, rows, :]], axis=0)
            product = lax.dot_general(
                left, stack[q, 0], (((1,), (1,)), ((), ())), preferred_element_type=jnp.float32
            )
            product = (product * norm).astype(jnp.bfloat16)
            out[q, 0, rows, :] = product[:128]
            out[q, 1, rows, :] = product[128:]

    for_each(inputs // 128, correlate)


def per_device(samples, taps):
    groups = lax.axis_size("inp")
    blocks = groups // BLOCK
    inputs = groups * INP_DEV
    table = jnp.asarray(dft_table(groups))
    frames = samples.reshape(INP_DEV, FRAMES, NFFT).transpose(1, 0, 2)
    anywhere = pl.BlockSpec(memory_space=pl.ANY)
    bf16, f32 = jnp.bfloat16, jnp.float32
    gathered = pl.pallas_call(
        functools.partial(kernel, groups),
        out_shape=pltpu.VMEM((groups, 2, BLOCK_ROWS, 128), bf16),
        in_specs=[pl.BlockSpec(memory_space=pltpu.HBM)] * 3,
        out_specs=pl.BlockSpec(memory_space=pltpu.VMEM),
        scratch_shapes=[
            pltpu.VMEM((2 * HALF_FRAMES, INP_DEV, NFFT), bf16),
            pltpu.VMEM((TAPS, NFFT), jnp.int32),
            pltpu.VMEM((blocks, NFFT, 2 * COLS), bf16),
            pltpu.VMEM((blocks, NFFT, TAPS * COLS), bf16),
            pltpu.VMEM((blocks, 2 * HALF_ROWS, TAPS * COLS), f32),
            pltpu.VMEM((HALF * INP_DEV, 128), f32),
            pltpu.VMEM((BLOCK_ROWS * BLOCK, 128), f32),
            pltpu.VMEM((groups, 2, BLOCK_ROWS, 128), bf16),
            pltpu.SemaphoreType.DMA((3,)),
            pltpu.SemaphoreType.DMA((2, len(LOADS))),
            pltpu.SemaphoreType.DMA((2,)),
            pltpu.SemaphoreType.DMA,
            pltpu.SemaphoreType.DMA,
        ],
        compiler_params=pltpu.CompilerParams(
            collective_id=0, has_side_effects=True, vmem_limit_bytes=58 * 2**20
        ),
        name="channelize",
    )(frames, taps, table)
    return pl.pallas_call(
        correlate_kernel,
        out_shape=jax.ShapeDtypeStruct((CH_DEV, 2, inputs, inputs), bf16),
        in_specs=[pl.BlockSpec(memory_space=pltpu.VMEM)],
        out_specs=pl.BlockSpec(memory_space=pltpu.VMEM),
        scratch_shapes=[pltpu.VMEM((CH_DEV, 2, inputs, 2 * SPEC), bf16)],
        compiler_params=pltpu.CompilerParams(vmem_limit_bytes=2**20 * (4 + groups // 4)),
        name="correlate",
    )(gathered)


def solution(mesh):
    placed = (P(("band", "inp"), None), P())
    return jax.shard_map(
        per_device,
        mesh=mesh,
        in_specs=placed,
        out_specs=P(("band", "inp"), None, None, None),
        check_vma=False,
    )
```

```python
import functools
import math

import jax
import jax.numpy as jnp
import numpy as np
from jax import lax
from jax.experimental import pallas as pl
from jax.experimental.pallas import tpu as pltpu
from jax.sharding import PartitionSpec as P

CH_DEV = 2
NFFT = 2048
TAPS = 4
FIRST_CH = 256
SPEC = 128
INP_DEV = 8
FRAMES = SPEC + TAPS - 1
BLOCK = 16
COLS = BLOCK * CH_DEV * 2
HALF = SPEC // 2
HALF_FRAMES = 68
HALF_ROWS = HALF_FRAMES * INP_DEV
LATE_FRAMES = FRAMES - HALF_FRAMES
LOADS = ((0, 32), (32, LATE_FRAMES - 32))
BLOCK_ROWS = CH_DEV * INP_DEV


def dft_table(groups):
    n = np.arange(NFFT, dtype=np.int64)[None, :, None]
    block = np.arange(groups // BLOCK)[:, None, None]
    column = np.arange(2 * COLS)[None, None, :] % COLS
    part = column // BLOCK
    channel = FIRST_CH + (block * BLOCK + column % BLOCK) * CH_DEV + part % CH_DEV
    phase = (n * channel % NFFT).astype(np.float32) * np.float32(2.0 * math.pi / NFFT)
    phase = phase.astype(np.float64)
    table = np.where(part < CH_DEV, np.cos(phase), -np.sin(phase)).astype(np.float32)
    return (table * np.float32(2.0**-19)).astype(jnp.bfloat16)


def for_each(count, body):
    if count == 1:
        body(0)
    else:
        pl.loop(0, count)(body)


def for_each_peer(groups, body):
    if groups <= BLOCK:
        for step in range(1, groups):
            body(step)
    else:
        pl.loop(1, groups)(body)


def kernel(
    groups, samples, taps, table, recv,
    x, taps_v, table_v, weights, prod, volts, turned, send,
    load_sem, sample_sem, own_sem, send_sem, recv_sem,
):
    me = lax.axis_index("inp")
    blocks = groups // BLOCK
    taps_copy = pltpu.make_async_copy(taps, taps_v, load_sem.at[0])
    table_copy = pltpu.make_async_copy(table, table_v, load_sem.at[1])
    taps_copy.start()
    table_copy.start()

    def load(first, count, sem):
        part = pl.ds(first, count)
        return pltpu.make_async_copy(samples.at[part], x.at[part], sem)

    extra = load(LATE_FRAMES, HALF_FRAMES - LATE_FRAMES, load_sem.at[2])
    for h in range(2):
        for index, (first, count) in enumerate(LOADS):
            load(h * HALF_FRAMES + first, count, sample_sem.at[h, index]).start()
        if h == 0:
            extra.start()

    barrier = pltpu.get_barrier_semaphore()

    def greet(step):
        peer = lax.rem(me + step, groups)
        pl.semaphore_signal(
            barrier, inc=1, device_id={"inp": peer}, device_id_type=pl.DeviceIdType.MESH
        )

    for_each_peer(groups, greet)

    width = TAPS * COLS
    tap_of = lax.broadcasted_iota(jnp.int32, (2 * TAPS, width), 1) // COLS
    spread = (tap_of == lax.broadcasted_iota(jnp.int32, (2 * TAPS, width), 0)).astype(jnp.bfloat16)
    taps_copy.wait()
    table_copy.wait()

    tap_rows = taps_v[...].astype(jnp.float32)
    tap_rows = jnp.concatenate([tap_rows, jnp.zeros_like(tap_rows)], axis=0).astype(jnp.bfloat16)
    spread_taps = lax.dot_general(
        tap_rows, spread, (((0,), (0,)), ((), ())), preferred_element_type=jnp.float32
    )

    def weigh(b):
        values = table_v[b].astype(jnp.float32)
        for h in range(2):
            lanes = slice(h * 2 * COLS, (h + 1) * 2 * COLS)
            weights[b, :, lanes] = (values * spread_taps[:, lanes]).astype(jnp.bfloat16)

    for_each(blocks, weigh)

    extra.wait()

    def transfer(peer, source, target):
        return pltpu.make_async_remote_copy(
            src_ref=source,
            dst_ref=target,
            send_sem=send_sem,
            recv_sem=recv_sem,
            device_id={"inp": peer},
            device_id_type=pl.DeviceIdType.MESH,
        )

    @pl.loop(0, 2)
    def _(h):
        for index, (first, count) in enumerate(LOADS):
            load(h * HALF_FRAMES + first, count, sample_sem.at[h, index]).wait()

        def multiply(b):
            rows = pl.ds(pl.multiple_of(h * HALF_ROWS, HALF_ROWS), HALF_ROWS)
            values = x[pl.ds(h * HALF_FRAMES, HALF_FRAMES)].reshape(HALF_ROWS, NFFT)
            prod[b, rows, :] = jnp.dot(values, weights[b], preferred_element_type=jnp.float32)

        for_each(blocks, multiply)

        def turn(b):
            count = HALF * INP_DEV
            start = pl.multiple_of(h * count, count)
            half = (
                prod[b, pl.ds(start, count + INP_DEV), 0:128]
                + prod[b, pl.ds(start + 2 * INP_DEV, count + INP_DEV), 128:256]
            )
            volts[...] = half[:count] + pltpu.roll(half[INP_DEV:], COLS, 1)
            low_lanes = lax.broadcasted_iota(jnp.int32, (HALF, 128), 1) < COLS
            for p in range(2):
                rows = []
                for ia in range(2):
                    i = 4 * ia + 2 * p
                    low = volts[pl.ds(i, HALF, stride=INP_DEV), :]
                    high = volts[pl.ds(i + 1, HALF, stride=INP_DEV), :]
                    rows.append(jnp.where(low_lanes, low, pltpu.roll(high, COLS, 1)))
                pair = jnp.concatenate(rows, axis=0).T
                for k in range(8):
                    to = ((k % 4) * 4 + 2 * p + k // 4) * BLOCK
                    turned[to : to + BLOCK, :] = pair[k * BLOCK : (k + 1) * BLOCK, :]
            first = lax.broadcasted_iota(jnp.int32, (INP_DEV, 128), 1) < HALF
            for g in range(BLOCK):
                real = turned[pl.ds(g, 8, stride=BLOCK), :]
                imag = turned[pl.ds(8 * BLOCK + g, 8, stride=BLOCK), :]
                send[b * BLOCK + g, h] = jnp.concatenate(
                    [
                        jnp.where(first, real, pltpu.roll(imag, HALF, 1)),
                        jnp.where(first, pltpu.roll(real, HALF, 1), imag),
                    ],
                    axis=0,
                ).astype(jnp.bfloat16)

        for_each(blocks, turn)

    pl.semaphore_wait(barrier, groups - 1)

    def start(step):
        peer = lax.rem(me + step, groups)
        transfer(peer, send.at[peer], recv.at[me]).start()

    for_each_peer(groups, start)
    own = pltpu.make_async_copy(send.at[me], recv.at[me], own_sem)
    own.start()
    own.wait()
    others = pl.ds(0, groups - 1)
    everything = transfer(lax.rem(me + 1, groups), send.at[others], recv.at[others])
    everything.wait_recv()
    everything.wait_send()


def correlate_kernel(recv, out, stack):
    inputs = recv.shape[0] * INP_DEV
    norm = 1.0 / math.sqrt(SPEC)
    shape = (recv.shape[0], INP_DEV, 128)
    upper = lax.broadcasted_iota(jnp.int32, shape, 1) < 4
    first = lax.broadcasted_iota(jnp.int32, (inputs, 128), 1) < HALF
    for h in range(2):
        lanes = slice(h * 128, (h + 1) * 128)
        early = recv[:, h, 0:INP_DEV, :].astype(jnp.float32)
        late = recv[:, h, INP_DEV:, :].astype(jnp.float32)
        by_channel = (
            jnp.where(upper, early, pltpu.roll(late, 4, 1)),
            jnp.where(upper, pltpu.roll(early, 4, 1), late),
        )
        for q in range(CH_DEV):
            values = by_channel[q].reshape(inputs, 128)
            rolled = pltpu.roll(values, HALF, 1)
            stack[q, 0, :, lanes] = values.astype(jnp.bfloat16)
            stack[q, 1, :, lanes] = jnp.where(first, rolled, -rolled).astype(jnp.bfloat16)

    def correlate(tile):
        rows = pl.ds(tile * 128, 128)
        for q in range(CH_DEV):
            for r in range(2):
                product = lax.dot_general(
                    stack[q, r, rows, :], stack[q, 0], (((1,), (1,)), ((), ())),
                    preferred_element_type=jnp.float32,
                )
                out[q, r, rows, :] = (product * norm).astype(jnp.bfloat16)

    for_each(inputs // 128, correlate)


def per_device(samples, taps):
    groups = lax.axis_size("inp")
    blocks = groups // BLOCK
    inputs = groups * INP_DEV
    table = jnp.asarray(dft_table(groups))
    frames = samples.reshape(INP_DEV, FRAMES, NFFT).transpose(1, 0, 2)
    anywhere = pl.BlockSpec(memory_space=pl.ANY)
    bf16, f32 = jnp.bfloat16, jnp.float32
    gathered = pl.pallas_call(
        functools.partial(kernel, groups),
        out_shape=pltpu.VMEM((groups, 2, BLOCK_ROWS, 128), bf16),
        in_specs=[pl.BlockSpec(memory_space=pltpu.HBM)] * 3,
        out_specs=pl.BlockSpec(memory_space=pltpu.VMEM),
        scratch_shapes=[
            pltpu.VMEM((2 * HALF_FRAMES, INP_DEV, NFFT), bf16),
            pltpu.VMEM((TAPS, NFFT), jnp.int32),
            pltpu.VMEM((blocks, NFFT, 2 * COLS), bf16),
            pltpu.VMEM((blocks, NFFT, TAPS * COLS), bf16),
            pltpu.VMEM((blocks, 2 * HALF_ROWS, TAPS * COLS), f32),
            pltpu.VMEM((HALF * INP_DEV, 128), f32),
            pltpu.VMEM((BLOCK_ROWS * BLOCK, 128), f32),
            pltpu.VMEM((groups, 2, BLOCK_ROWS, 128), bf16),
            pltpu.SemaphoreType.DMA((3,)),
            pltpu.SemaphoreType.DMA((2, len(LOADS))),
            pltpu.SemaphoreType.DMA,
            pltpu.SemaphoreType.DMA,
            pltpu.SemaphoreType.DMA,
        ],
        compiler_params=pltpu.CompilerParams(
            collective_id=0, has_side_effects=True, vmem_limit_bytes=58 * 2**20
        ),
        name="channelize",
    )(frames, taps, table)
    return pl.pallas_call(
        correlate_kernel,
        out_shape=jax.ShapeDtypeStruct((CH_DEV, 2, inputs, inputs), bf16),
        in_specs=[pl.BlockSpec(memory_space=pltpu.VMEM)],
        out_specs=pl.BlockSpec(memory_space=pltpu.VMEM),
        scratch_shapes=[pltpu.VMEM((CH_DEV, 2, inputs, 2 * SPEC), bf16)],
        compiler_params=pltpu.CompilerParams(vmem_limit_bytes=2**20 * (4 + groups // 4)),
        name="correlate",
    )(gathered)


def solution(mesh):
    placed = (P(("band", "inp"), None), P())
    return jax.shard_map(
        per_device,
        mesh=mesh,
        in_specs=placed,
        out_specs=P(("band", "inp"), None, None, None),
        check_vma=False,
    )
```

```python
import functools
import math

import jax
import jax.numpy as jnp
import numpy as np
from jax import lax
from jax.experimental import pallas as pl
from jax.experimental.pallas import tpu as pltpu
from jax.sharding import PartitionSpec as P

CH_DEV = 2
NFFT = 2048
TAPS = 4
FIRST_CH = 256
SPEC = 128
INP_DEV = 8
FRAMES = SPEC + TAPS - 1
BLOCK = 16
COLS = BLOCK * CH_DEV * 2
HALF_FRAMES = 68
HALF_ROWS = HALF_FRAMES * INP_DEV
LATE_FRAMES = FRAMES - HALF_FRAMES
LOADS = ((0, 32), (32, LATE_FRAMES - 32))
BLOCK_ROWS = CH_DEV * 2 * INP_DEV


def dft_table(groups):
    n = np.arange(NFFT, dtype=np.int64)[None, :, None]
    block = np.arange(groups // BLOCK)[:, None, None]
    column = np.arange(2 * COLS)[None, None, :] % COLS
    part = column // BLOCK
    channel = FIRST_CH + (block * BLOCK + column % BLOCK) * CH_DEV + part // 2
    phase = (n * channel % NFFT).astype(np.float32) * np.float32(2.0 * math.pi / NFFT)
    phase = phase.astype(np.float64)
    table = np.where(part % 2 == 0, np.cos(phase), -np.sin(phase)).astype(np.float32)
    return (table * np.float32(2.0**-19)).astype(jnp.bfloat16)


def for_each(count, body):
    if count == 1:
        body(0)
    else:
        pl.loop(0, count)(body)


def for_each_peer(groups, body):
    if groups <= BLOCK:
        for step in range(1, groups):
            body(step)
    else:
        pl.loop(1, groups)(body)


def kernel(
    groups, samples, taps, table, recv,
    x, taps_v, table_v, weights, prod, volts, turned, send,
    load_sem, sample_sem, own_sem, send_sem, recv_sem,
):
    me = lax.axis_index("inp")
    blocks = groups // BLOCK
    taps_copy = pltpu.make_async_copy(taps, taps_v, load_sem.at[0])
    table_copy = pltpu.make_async_copy(table, table_v, load_sem.at[1])
    taps_copy.start()
    table_copy.start()

    def load(first, count, sem):
        part = pl.ds(first, count)
        return pltpu.make_async_copy(samples.at[part], x.at[part], sem)

    extra = load(LATE_FRAMES, HALF_FRAMES - LATE_FRAMES, load_sem.at[2])
    for h in range(2):
        for index, (first, count) in enumerate(LOADS):
            load(h * HALF_FRAMES + first, count, sample_sem.at[h, index]).start()
        if h == 0:
            extra.start()

    barrier = pltpu.get_barrier_semaphore()

    def greet(step):
        peer = lax.rem(me + step, groups)
        pl.semaphore_signal(
            barrier, inc=1, device_id={"inp": peer}, device_id_type=pl.DeviceIdType.MESH
        )

    for_each_peer(groups, greet)

    width = TAPS * COLS
    tap_of = lax.broadcasted_iota(jnp.int32, (2 * TAPS, width), 1) // COLS
    spread = (tap_of == lax.broadcasted_iota(jnp.int32, (2 * TAPS, width), 0)).astype(jnp.bfloat16)
    taps_copy.wait()
    table_copy.wait()

    tap_rows = taps_v[...].astype(jnp.float32)
    tap_rows = jnp.concatenate([tap_rows, jnp.zeros_like(tap_rows)], axis=0).astype(jnp.bfloat16)
    spread_taps = lax.dot_general(
        tap_rows, spread, (((0,), (0,)), ((), ())), preferred_element_type=jnp.float32
    )

    def weigh(b):
        values = table_v[b].astype(jnp.float32)
        for h in range(2):
            lanes = slice(h * 2 * COLS, (h + 1) * 2 * COLS)
            weights[b, :, lanes] = (values * spread_taps[:, lanes]).astype(jnp.bfloat16)

    for_each(blocks, weigh)

    extra.wait()

    def transfer(peer, source, target):
        return pltpu.make_async_remote_copy(
            src_ref=source,
            dst_ref=target,
            send_sem=send_sem,
            recv_sem=recv_sem,
            device_id={"inp": peer},
            device_id_type=pl.DeviceIdType.MESH,
        )

    @pl.loop(0, 2)
    def _(h):
        for index, (first, count) in enumerate(LOADS):
            load(h * HALF_FRAMES + first, count, sample_sem.at[h, index]).wait()

        def multiply(b):
            rows = pl.ds(pl.multiple_of(h * HALF_ROWS, HALF_ROWS), HALF_ROWS)
            values = x[pl.ds(h * HALF_FRAMES, HALF_FRAMES)].reshape(HALF_ROWS, NFFT)
            prod[b, rows, :] = jnp.dot(values, weights[b], preferred_element_type=jnp.float32)

        for_each(blocks, multiply)

    def turn(b):
        count = SPEC * INP_DEV
        half = prod[b, 0 : count + INP_DEV, 0:128] + prod[b, 16 : count + 24, 128:256]
        volts[...] = half[:count] + pltpu.roll(half[INP_DEV:], COLS, 1)
        lane = lax.broadcasted_iota(jnp.int32, (SPEC, 128), 1)
        for i in range(INP_DEV // 2):
            low = volts[pl.ds(i, SPEC, stride=INP_DEV), :]
            high = volts[pl.ds(i + 4, SPEC, stride=INP_DEV), :]
            pair = jnp.where(lane < COLS, low, pltpu.roll(high, COLS, 1)).T
            for k in range(8):
                to = (k % 4) * INP_DEV * BLOCK + (i + 4 * (k // 4)) * BLOCK
                turned[to : to + BLOCK, :] = pair[k * BLOCK : (k + 1) * BLOCK, :]
        for g in range(BLOCK):
            send[b * BLOCK + g] = turned[pl.ds(g, BLOCK_ROWS, stride=BLOCK), :].astype(jnp.bfloat16)

    for_each(blocks, turn)

    pl.semaphore_wait(barrier, groups - 1)

    def start(step):
        peer = lax.rem(me + step, groups)
        transfer(peer, send.at[peer], recv.at[me]).start()

    for_each_peer(groups, start)
    own = pltpu.make_async_copy(send.at[me], recv.at[me], own_sem)
    own.start()
    own.wait()
    others = pl.ds(0, groups - 1)
    everything = transfer(lax.rem(me + 1, groups), send.at[others], recv.at[others])
    everything.wait_recv()
    everything.wait_send()


def correlate_kernel(recv, out, stack):
    inputs = recv.shape[0] * INP_DEV
    norm = 1.0 / math.sqrt(SPEC)
    for q in range(CH_DEV):
        for r in range(2):
            at = (2 * q + r) * INP_DEV
            values = recv[:, at : at + INP_DEV, :].astype(jnp.float32).reshape(inputs, SPEC)
            stack[q, 0, :, r * SPEC : (r + 1) * SPEC] = values.astype(jnp.bfloat16)
            turned_part = values if r == 1 else -values
            stack[q, 1, :, (1 - r) * SPEC : (2 - r) * SPEC] = turned_part.astype(jnp.bfloat16)

    def correlate(tile):
        rows = pl.ds(tile * SPEC, SPEC)
        for q in range(CH_DEV):
            for r in range(2):
                product = lax.dot_general(
                    stack[q, r, rows, :], stack[q, 0], (((1,), (1,)), ((), ())),
                    preferred_element_type=jnp.float32,
                )
                out[q, r, rows, :] = (product * norm).astype(jnp.bfloat16)

    for_each(inputs // SPEC, correlate)


def per_device(samples, taps):
    groups = lax.axis_size("inp")
    blocks = groups // BLOCK
    inputs = groups * INP_DEV
    table = jnp.asarray(dft_table(groups))
    frames = samples.reshape(INP_DEV, FRAMES, NFFT).transpose(1, 0, 2)
    anywhere = pl.BlockSpec(memory_space=pl.ANY)
    bf16, f32 = jnp.bfloat16, jnp.float32
    gathered = pl.pallas_call(
        functools.partial(kernel, groups),
        out_shape=pltpu.VMEM((groups, BLOCK_ROWS, SPEC), bf16),
        in_specs=[pl.BlockSpec(memory_space=pltpu.HBM)] * 3,
        out_specs=pl.BlockSpec(memory_space=pltpu.VMEM),
        scratch_shapes=[
            pltpu.VMEM((2 * HALF_FRAMES, INP_DEV, NFFT), bf16),
            pltpu.VMEM((TAPS, NFFT), jnp.int32),
            pltpu.VMEM((blocks, NFFT, 2 * COLS), bf16),
            pltpu.VMEM((blocks, NFFT, TAPS * COLS), bf16),
            pltpu.VMEM((blocks, 2 * HALF_ROWS, TAPS * COLS), f32),
            pltpu.VMEM((SPEC * INP_DEV, 128), f32),
            pltpu.VMEM((BLOCK_ROWS * BLOCK, SPEC), f32),
            pltpu.VMEM((groups, BLOCK_ROWS, SPEC), bf16),
            pltpu.SemaphoreType.DMA((3,)),
            pltpu.SemaphoreType.DMA((2, len(LOADS))),
            pltpu.SemaphoreType.DMA,
            pltpu.SemaphoreType.DMA,
            pltpu.SemaphoreType.DMA,
        ],
        compiler_params=pltpu.CompilerParams(
            collective_id=0, has_side_effects=True, vmem_limit_bytes=58 * 2**20
        ),
        name="channelize",
    )(frames, taps, table)
    return pl.pallas_call(
        correlate_kernel,
        out_shape=jax.ShapeDtypeStruct((CH_DEV, 2, inputs, inputs), bf16),
        in_specs=[pl.BlockSpec(memory_space=pltpu.VMEM)],
        out_specs=pl.BlockSpec(memory_space=pltpu.VMEM),
        scratch_shapes=[pltpu.VMEM((CH_DEV, 2, inputs, 2 * SPEC), bf16)],
        compiler_params=pltpu.CompilerParams(vmem_limit_bytes=2**20 * (4 + groups // 4)),
        name="correlate",
    )(gathered)


def solution(mesh):
    placed = (P(("band", "inp"), None), P())
    return jax.shard_map(
        per_device,
        mesh=mesh,
        in_specs=placed,
        out_specs=P(("band", "inp"), None, None, None),
        check_vma=False,
    )
```

```python
import functools
import math

import jax
import jax.numpy as jnp
import numpy as np
from jax import lax
from jax.experimental import pallas as pl
from jax.experimental.pallas import tpu as pltpu
from jax.sharding import PartitionSpec as P

CH_DEV = 2
NFFT = 2048
TAPS = 4
FIRST_CH = 256
SPEC = 128
INP_DEV = 8
FRAMES = SPEC + TAPS - 1
BLOCK = 16
COLS = BLOCK * CH_DEV * 2
HALF_FRAMES = 68
HALF_ROWS = HALF_FRAMES * INP_DEV
LATE_FRAMES = FRAMES - HALF_FRAMES
LOADS = tuple((first, min(8, LATE_FRAMES - first)) for first in range(0, LATE_FRAMES, 8))
BLOCK_ROWS = CH_DEV * 2 * INP_DEV


def dft_table(groups):
    n = np.arange(NFFT, dtype=np.int64)[None, :, None]
    block = np.arange(groups // BLOCK)[:, None, None]
    column = np.arange(2 * COLS)[None, None, :] % COLS
    part = column // BLOCK
    channel = FIRST_CH + (block * BLOCK + column % BLOCK) * CH_DEV + part // 2
    phase = (n * channel % NFFT).astype(np.float32) * np.float32(2.0 * math.pi / NFFT)
    phase = phase.astype(np.float64)
    table = np.where(part % 2 == 0, np.cos(phase), -np.sin(phase)).astype(np.float32)
    return (table * np.float32(2.0**-19)).astype(jnp.bfloat16)


def for_each(count, body):
    if count == 1:
        body(0)
    else:
        pl.loop(0, count)(body)


def for_each_peer(groups, body):
    if groups <= BLOCK:
        for step in range(1, groups):
            body(step)
    else:
        pl.loop(1, groups)(body)


def kernel(
    groups, samples, taps, table, recv,
    x, taps_v, table_v, weights, prod, volts, turned, send,
    load_sem, sample_sem, own_sem, send_sem, recv_sem,
):
    me = lax.axis_index("inp")
    blocks = groups // BLOCK
    taps_copy = pltpu.make_async_copy(taps, taps_v, load_sem.at[0])
    table_copy = pltpu.make_async_copy(table, table_v, load_sem.at[1])
    taps_copy.start()
    table_copy.start()

    def load(first, count, sem):
        part = pl.ds(first, count)
        return pltpu.make_async_copy(samples.at[part], x.at[part], sem)

    extra = load(LATE_FRAMES, HALF_FRAMES - LATE_FRAMES, load_sem.at[2])
    for h in range(2):
        for index, (first, count) in enumerate(LOADS):
            load(h * HALF_FRAMES + first, count, sample_sem.at[h, index]).start()
        if h == 0:
            extra.start()

    barrier = pltpu.get_barrier_semaphore()

    def greet(step):
        peer = lax.rem(me + step, groups)
        pl.semaphore_signal(
            barrier, inc=1, device_id={"inp": peer}, device_id_type=pl.DeviceIdType.MESH
        )

    for_each_peer(groups, greet)

    width = TAPS * COLS
    tap_of = lax.broadcasted_iota(jnp.int32, (2 * TAPS, width), 1) // COLS
    spread = (tap_of == lax.broadcasted_iota(jnp.int32, (2 * TAPS, width), 0)).astype(jnp.bfloat16)
    taps_copy.wait()
    table_copy.wait()

    tap_rows = taps_v[...].astype(jnp.float32)
    tap_rows = jnp.concatenate([tap_rows, jnp.zeros_like(tap_rows)], axis=0).astype(jnp.bfloat16)
    spread_taps = lax.dot_general(
        tap_rows, spread, (((0,), (0,)), ((), ())), preferred_element_type=jnp.float32
    )

    def weigh(b):
        values = table_v[b].astype(jnp.float32)
        for h in range(2):
            lanes = slice(h * 2 * COLS, (h + 1) * 2 * COLS)
            weights[b, :, lanes] = (values * spread_taps[:, lanes]).astype(jnp.bfloat16)

    for_each(blocks, weigh)

    extra.wait()

    def transfer(peer, source, target):
        return pltpu.make_async_remote_copy(
            src_ref=source,
            dst_ref=target,
            send_sem=send_sem,
            recv_sem=recv_sem,
            device_id={"inp": peer},
            device_id_type=pl.DeviceIdType.MESH,
        )

    @pl.loop(0, 2)
    def _(h):
        for index, (first, count) in enumerate(LOADS):
            load(h * HALF_FRAMES + first, count, sample_sem.at[h, index]).wait()

        def multiply(b):
            rows = pl.ds(pl.multiple_of(h * HALF_ROWS, HALF_ROWS), HALF_ROWS)
            values = x[pl.ds(h * HALF_FRAMES, HALF_FRAMES)].reshape(HALF_ROWS, NFFT)
            prod[b, rows, :] = jnp.dot(values, weights[b], preferred_element_type=jnp.float32)

        for_each(blocks, multiply)

    def turn(b):
        count = SPEC * INP_DEV
        half = prod[b, 0 : count + INP_DEV, 0:128] + prod[b, 16 : count + 24, 128:256]
        volts[...] = half[:count] + pltpu.roll(half[INP_DEV:], COLS, 1)
        lane = lax.broadcasted_iota(jnp.int32, (SPEC, 128), 1)
        for i in range(INP_DEV // 2):
            low = volts[pl.ds(i, SPEC, stride=INP_DEV), :]
            high = volts[pl.ds(i + 4, SPEC, stride=INP_DEV), :]
            pair = jnp.where(lane < COLS, low, pltpu.roll(high, COLS, 1)).T
            for k in range(8):
                to = (k % 4) * INP_DEV * BLOCK + (i + 4 * (k // 4)) * BLOCK
                turned[to : to + BLOCK, :] = pair[k * BLOCK : (k + 1) * BLOCK, :]
        if blocks > 1:
            for g in range(BLOCK):
                fill(b * BLOCK + g, g)

    def fill(group, g):
        rows = turned[pl.ds(g, BLOCK_ROWS, stride=BLOCK), :]
        send[group] = rows.astype(jnp.bfloat16)

    for_each(blocks, turn)

    pl.semaphore_wait(barrier, groups - 1)

    def start(step):
        peer = lax.rem(me + step, groups)
        if blocks == 1:
            fill(peer, peer)
        transfer(peer, send.at[peer], recv.at[me]).start()

    for_each_peer(groups, start)
    if blocks == 1:
        fill(me, me)
    own = pltpu.make_async_copy(send.at[me], recv.at[me], own_sem)
    own.start()
    own.wait()
    others = pl.ds(0, groups - 1)
    everything = transfer(lax.rem(me + 1, groups), send.at[others], recv.at[others])
    everything.wait_recv()
    everything.wait_send()


def correlate_kernel(recv, out, stack):
    inputs = recv.shape[0] * INP_DEV
    norm = 1.0 / math.sqrt(SPEC)
    for q in range(CH_DEV):
        for r in range(2):
            at = (2 * q + r) * INP_DEV
            values = recv[:, at : at + INP_DEV, :].astype(jnp.float32).reshape(inputs, SPEC)
            stack[q, 0, :, r * SPEC : (r + 1) * SPEC] = values.astype(jnp.bfloat16)
            turned_part = values if r == 1 else -values
            stack[q, 1, :, (1 - r) * SPEC : (2 - r) * SPEC] = turned_part.astype(jnp.bfloat16)

    def correlate(tile):
        rows = pl.ds(tile * SPEC, SPEC)
        for q in range(CH_DEV):
            for r in range(2):
                product = lax.dot_general(
                    stack[q, r, rows, :], stack[q, 0], (((1,), (1,)), ((), ())),
                    preferred_element_type=jnp.float32,
                )
                out[q, r, rows, :] = (product * norm).astype(jnp.bfloat16)

    for_each(inputs // SPEC, correlate)


def per_device(samples, taps):
    groups = lax.axis_size("inp")
    blocks = groups // BLOCK
    inputs = groups * INP_DEV
    table = jnp.asarray(dft_table(groups))
    frames = samples.reshape(INP_DEV, FRAMES, NFFT).transpose(1, 0, 2)
    anywhere = pl.BlockSpec(memory_space=pl.ANY)
    bf16, f32 = jnp.bfloat16, jnp.float32
    gathered = pl.pallas_call(
        functools.partial(kernel, groups),
        out_shape=pltpu.VMEM((groups, BLOCK_ROWS, SPEC), bf16),
        in_specs=[pl.BlockSpec(memory_space=pltpu.HBM)] * 3,
        out_specs=pl.BlockSpec(memory_space=pltpu.VMEM),
        scratch_shapes=[
            pltpu.VMEM((2 * HALF_FRAMES, INP_DEV, NFFT), bf16),
            pltpu.VMEM((TAPS, NFFT), jnp.int32),
            pltpu.VMEM((blocks, NFFT, 2 * COLS), bf16),
            pltpu.VMEM((blocks, NFFT, TAPS * COLS), bf16),
            pltpu.VMEM((blocks, 2 * HALF_ROWS, TAPS * COLS), f32),
            pltpu.VMEM((SPEC * INP_DEV, 128), f32),
            pltpu.VMEM((BLOCK_ROWS * BLOCK, SPEC), f32),
            pltpu.VMEM((groups, BLOCK_ROWS, SPEC), bf16),
            pltpu.SemaphoreType.DMA((3,)),
            pltpu.SemaphoreType.DMA((2, len(LOADS))),
            pltpu.SemaphoreType.DMA,
            pltpu.SemaphoreType.DMA,
            pltpu.SemaphoreType.DMA,
        ],
        compiler_params=pltpu.CompilerParams(
            collective_id=0, has_side_effects=True, vmem_limit_bytes=58 * 2**20
        ),
        name="channelize",
    )(frames, taps, table)
    return pl.pallas_call(
        correlate_kernel,
        out_shape=jax.ShapeDtypeStruct((CH_DEV, 2, inputs, inputs), bf16),
        in_specs=[pl.BlockSpec(memory_space=pltpu.VMEM)],
        out_specs=pl.BlockSpec(memory_space=pltpu.VMEM),
        scratch_shapes=[pltpu.VMEM((CH_DEV, 2, inputs, 2 * SPEC), bf16)],
        compiler_params=pltpu.CompilerParams(vmem_limit_bytes=2**20 * (4 + groups // 4)),
        name="correlate",
    )(gathered)


def solution(mesh):
    placed = (P(("band", "inp"), None), P())
    return jax.shard_map(
        per_device,
        mesh=mesh,
        in_specs=placed,
        out_specs=P(("band", "inp"), None, None, None),
        check_vma=False,
    )
```

```python
import functools
import math

import jax
import jax.numpy as jnp
import numpy as np
from jax import lax
from jax.experimental import pallas as pl
from jax.experimental.pallas import tpu as pltpu
from jax.sharding import PartitionSpec as P

CH_DEV = 2
NFFT = 2048
TAPS = 4
FIRST_CH = 256
SPEC = 128
INP_DEV = 8
FRAMES = SPEC + TAPS - 1
BLOCK = 16
COLS = BLOCK * CH_DEV * 2
HALF_FRAMES = 68
HALF_ROWS = HALF_FRAMES * INP_DEV
LATE_FRAMES = FRAMES - HALF_FRAMES
LOADS = ((0, 32), (32, LATE_FRAMES - 32))
BLOCK_ROWS = CH_DEV * 2 * INP_DEV


def dft_table(groups):
    n = np.arange(NFFT, dtype=np.int64)[None, :, None]
    block = np.arange(groups // BLOCK)[:, None, None]
    column = np.arange(2 * COLS)[None, None, :] % COLS
    part = column // BLOCK
    channel = FIRST_CH + (block * BLOCK + column % BLOCK) * CH_DEV + part // 2
    phase = (n * channel % NFFT).astype(np.float32) * np.float32(2.0 * math.pi / NFFT)
    phase = phase.astype(np.float64)
    table = np.where(part % 2 == 0, np.cos(phase), -np.sin(phase)).astype(np.float32)
    return (table * np.float32(2.0**-19)).astype(jnp.bfloat16)


def for_each(count, body):
    if count == 1:
        body(0)
    else:
        pl.loop(0, count)(body)


def for_each_peer(groups, body):
    if groups <= BLOCK:
        for step in range(1, groups):
            body(step)
    else:
        pl.loop(1, groups)(body)


def kernel(
    groups, samples, taps, table, recv,
    x, taps_v, table_v, weights, prod, volts, turned, send,
    load_sem, sample_sem, own_sem, send_sem, recv_sem,
):
    me = lax.axis_index("inp")
    blocks = groups // BLOCK
    taps_copy = pltpu.make_async_copy(taps, taps_v, load_sem.at[0])
    table_copy = pltpu.make_async_copy(table, table_v, load_sem.at[1])
    taps_copy.start()
    table_copy.start()

    def load(first, count, sem):
        part = pl.ds(first, count)
        return pltpu.make_async_copy(samples.at[part], x.at[part], sem)

    extra = load(LATE_FRAMES, HALF_FRAMES - LATE_FRAMES, load_sem.at[2])
    for h in range(2):
        for index, (first, count) in enumerate(LOADS):
            load(h * HALF_FRAMES + first, count, sample_sem.at[h, index]).start()
        if h == 0:
            extra.start()

    barrier = pltpu.get_barrier_semaphore()

    def greet(step):
        peer = lax.rem(me + step, groups)
        pl.semaphore_signal(
            barrier, inc=1, device_id={"inp": peer}, device_id_type=pl.DeviceIdType.MESH
        )

    for_each_peer(groups, greet)

    width = TAPS * COLS
    tap_of = lax.broadcasted_iota(jnp.int32, (2 * TAPS, width), 1) // COLS
    spread = (tap_of == lax.broadcasted_iota(jnp.int32, (2 * TAPS, width), 0)).astype(jnp.bfloat16)
    taps_copy.wait()
    table_copy.wait()

    tap_rows = taps_v[...].astype(jnp.float32)
    tap_rows = jnp.concatenate([tap_rows, jnp.zeros_like(tap_rows)], axis=0).astype(jnp.bfloat16)
    spread_taps = lax.dot_general(
        tap_rows, spread, (((0,), (0,)), ((), ())), preferred_element_type=jnp.float32
    ).astype(jnp.bfloat16)

    def weigh(b):
        for h in range(2):
            lanes = slice(h * 2 * COLS, (h + 1) * 2 * COLS)
            weights[b, :, lanes] = table_v[b] * spread_taps[:, lanes]

    for_each(blocks, weigh)

    extra.wait()

    def transfer(peer, source, target):
        return pltpu.make_async_remote_copy(
            src_ref=source,
            dst_ref=target,
            send_sem=send_sem,
            recv_sem=recv_sem,
            device_id={"inp": peer},
            device_id_type=pl.DeviceIdType.MESH,
        )

    @pl.loop(0, 2)
    def _(h):
        for index, (first, count) in enumerate(LOADS):
            load(h * HALF_FRAMES + first, count, sample_sem.at[h, index]).wait()

        def multiply(b):
            rows = pl.ds(pl.multiple_of(h * HALF_ROWS, HALF_ROWS), HALF_ROWS)
            values = x[pl.ds(h * HALF_FRAMES, HALF_FRAMES)].reshape(HALF_ROWS, NFFT)
            prod[b, rows, :] = jnp.dot(values, weights[b], preferred_element_type=jnp.float32)

        for_each(blocks, multiply)

    def turn(b):
        count = SPEC * INP_DEV
        half = prod[b, 0 : count + INP_DEV, 0:128] + prod[b, 16 : count + 24, 128:256]
        volts[...] = half[:count] + pltpu.roll(half[INP_DEV:], COLS, 1)
        lane = lax.broadcasted_iota(jnp.int32, (SPEC, 128), 1)
        for i in range(INP_DEV // 2):
            low = volts[pl.ds(i, SPEC, stride=INP_DEV), :]
            high = volts[pl.ds(i + 4, SPEC, stride=INP_DEV), :]
            pair = jnp.where(lane < COLS, low, pltpu.roll(high, COLS, 1)).T
            for k in range(8):
                to = (k % 4) * INP_DEV * BLOCK + (i + 4 * (k // 4)) * BLOCK
                turned[to : to + BLOCK, :] = pair[k * BLOCK : (k + 1) * BLOCK, :]
        for g in range(BLOCK):
            send[b * BLOCK + g] = turned[pl.ds(g, BLOCK_ROWS, stride=BLOCK), :].astype(jnp.bfloat16)

    for_each(blocks, turn)

    pl.semaphore_wait(barrier, groups - 1)

    def start(step):
        peer = lax.rem(me + step, groups)
        transfer(peer, send.at[peer], recv.at[me]).start()

    for_each_peer(groups, start)
    own = pltpu.make_async_copy(send.at[me], recv.at[me], own_sem)
    own.start()
    own.wait()
    others = pl.ds(0, groups - 1)
    everything = transfer(lax.rem(me + 1, groups), send.at[others], recv.at[others])
    everything.wait_recv()
    everything.wait_send()


def correlate_kernel(recv, out, stack):
    inputs = recv.shape[0] * INP_DEV
    norm = 1.0 / math.sqrt(SPEC)
    for q in range(CH_DEV):
        for r in range(2):
            at = (2 * q + r) * INP_DEV
            values = recv[:, at : at + INP_DEV, :].astype(jnp.float32).reshape(inputs, SPEC)
            stack[q, 0, :, r * SPEC : (r + 1) * SPEC] = values.astype(jnp.bfloat16)
            turned_part = values if r == 1 else -values
            stack[q, 1, :, (1 - r) * SPEC : (2 - r) * SPEC] = turned_part.astype(jnp.bfloat16)

    def correlate(tile):
        rows = pl.ds(tile * SPEC, SPEC)
        for q in range(CH_DEV):
            for r in range(2):
                product = lax.dot_general(
                    stack[q, r, rows, :], stack[q, 0], (((1,), (1,)), ((), ())),
                    preferred_element_type=jnp.float32,
                )
                out[q, r, rows, :] = (product * norm).astype(jnp.bfloat16)

    for_each(inputs // SPEC, correlate)


def per_device(samples, taps):
    groups = lax.axis_size("inp")
    blocks = groups // BLOCK
    inputs = groups * INP_DEV
    table = jnp.asarray(dft_table(groups))
    frames = samples.reshape(INP_DEV, FRAMES, NFFT).transpose(1, 0, 2)
    anywhere = pl.BlockSpec(memory_space=pl.ANY)
    bf16, f32 = jnp.bfloat16, jnp.float32
    gathered = pl.pallas_call(
        functools.partial(kernel, groups),
        out_shape=pltpu.VMEM((groups, BLOCK_ROWS, SPEC), bf16),
        in_specs=[pl.BlockSpec(memory_space=pltpu.HBM)] * 3,
        out_specs=pl.BlockSpec(memory_space=pltpu.VMEM),
        scratch_shapes=[
            pltpu.VMEM((2 * HALF_FRAMES, INP_DEV, NFFT), bf16),
            pltpu.VMEM((TAPS, NFFT), jnp.int32),
            pltpu.VMEM((blocks, NFFT, 2 * COLS), bf16),
            pltpu.VMEM((blocks, NFFT, TAPS * COLS), bf16),
            pltpu.VMEM((blocks, 2 * HALF_ROWS, TAPS * COLS), f32),
            pltpu.VMEM((SPEC * INP_DEV, 128), f32),
            pltpu.VMEM((BLOCK_ROWS * BLOCK, SPEC), f32),
            pltpu.VMEM((groups, BLOCK_ROWS, SPEC), bf16),
            pltpu.SemaphoreType.DMA((3,)),
            pltpu.SemaphoreType.DMA((2, len(LOADS))),
            pltpu.SemaphoreType.DMA,
            pltpu.SemaphoreType.DMA,
            pltpu.SemaphoreType.DMA,
        ],
        compiler_params=pltpu.CompilerParams(
            collective_id=0, has_side_effects=True, vmem_limit_bytes=58 * 2**20
        ),
        name="channelize",
    )(frames, taps, table)
    return pl.pallas_call(
        correlate_kernel,
        out_shape=jax.ShapeDtypeStruct((CH_DEV, 2, inputs, inputs), bf16),
        in_specs=[pl.BlockSpec(memory_space=pltpu.VMEM)],
        out_specs=pl.BlockSpec(memory_space=pltpu.VMEM),
        scratch_shapes=[pltpu.VMEM((CH_DEV, 2, inputs, 2 * SPEC), bf16)],
        compiler_params=pltpu.CompilerParams(vmem_limit_bytes=2**20 * (4 + groups // 4)),
        name="correlate",
    )(gathered)


def solution(mesh):
    placed = (P(("band", "inp"), None), P())
    return jax.shard_map(
        per_device,
        mesh=mesh,
        in_specs=placed,
        out_specs=P(("band", "inp"), None, None, None),
        check_vma=False,
    )
```
